32 devices in a mesh: arch: 2 (over core), dom: 16 (over z, y, x).
Axes of the slice: x: 2, y: 2, z: 4, core: 2. Of those that a mesh axis runs over, the one named last changes fastest.
Arguments:
- position: float32 [3, 131072], P(None, ('arch', 'dom')), may hold values from -6 to 6
- particle_mass: float32 [131072], P(('arch', 'dom')), may hold values from 0.5 to 2
- settling: float32 [131072], P(('arch', 'dom')), may hold values from 0.05 to 1
- walk_noise: float32 [3, 3, 131072], P(None, None, ('arch', 'dom')), may hold values from -6 to 6
- velocity: bfloat16 [4, 3, 32, 2048], P(None, None, ('arch', 'dom')), may hold values from -6 to 6
- diffusivity: bfloat16 [4, 32, 2048], P(None, ('arch', 'dom')), may hold values from 0.019897461 to 0.5
- block_tile: int32 [3, 32, 16], P(None, ('arch', 'dom')), may hold values from 0 to 31, as said below
- cell_index: int32 [3, 131072], P(None, ('arch', 'dom')), may hold values from 0 to 2047
- bed_cell: int32 [3, 131072], P(None, ('arch', 'dom')), may hold values from 0 to 511
- route_code: int32 [2, 32, 16], P(None, ('arch', 'dom')), may hold values from 0 to 15, each once within a row
Outputs:
- final_position: float32 [3, 131072], P(None, ('arch', 'dom'))
- final_mass: float32 [131072], P(('arch', 'dom'))
- bed_deposit: float32 [32, 512], P(('arch', 'dom'))
The draws below stay inside these ranges and needn't reach their ends.
Inputs may be any that keep to these rules, and one draw needn't show every extreme that they name: `block_tile`: in every step each block's tile belongs to the group of the block's dom index d: (tile) % 16 equals d. Within each group, tiles held at lower arch indices are used by more blocks than those at higher ones.
All inputs are finite; a program needn't handle non-finite values.
Results may differ from the reference program's by a relative error of at most 0.0003.
Values may be sent and summed in bfloat16 or wider, within the bound.
A program may use at most 64 MiB of HBM per device.

```python
import math
import jax
import jax.numpy as jnp

BLOCK = 256
BLK_PEER = 1
STEPS = 3
TILE_ARCH = 1
CELLS = 2048
BEDC = 512
SLABS = 4
NB = 16
PART_DEV = 4096
PARTICLES = 131072
NT = 32
N_ARCH = 2
N_DOM = 16
DEVICES = 32


def draw_block_tile(key, part):
    keyed = jax.random.fold_in(key, 7)
    key_one, key_two, key_three = jax.random.split(keyed, 3)
    shape = (STEPS, DEVICES, NB)
    owner_one = jax.random.randint(key_one, shape, 0, N_ARCH)
    owner_two = jax.random.randint(key_two, shape, 0, N_ARCH)
    owner = jnp.minimum(owner_one, owner_two)
    within = jax.random.randint(key_three, shape, 0, TILE_ARCH)
    dom_ids = (jnp.arange(DEVICES, dtype=jnp.int32) % N_DOM)[None, :, None]
    tiles = (owner * N_DOM + dom_ids) * TILE_ARCH + within
    tiles = tiles.at[0, DEVICES - 1, 0].set(NT - 1)
    tiles = tiles.at[0, 0, 0].set(0)
    return tiles.astype(jnp.int32)


def touch_ends(array, rng, least, largest):
    shape = array.shape
    index_at = [jax.random.randint(jax.random.fold_in(rng, axis), (), 0, shape[axis]) for axis in range(len(shape))]
    array = array.at[tuple(index_at)].set(least)
    longest = shape.index(max(shape))
    index_at[longest] = (index_at[longest] + 1) % shape[longest]
    return array.at[tuple(index_at)].set(largest)


def level_of(stream_key, dims, shards, smallest, largest):
    def one(axis_at, blocks):
        heights = jax.random.uniform(jax.random.fold_in(jax.random.fold_in(stream_key, 6), axis_at), (blocks,), jnp.float32, smallest / len(shards), largest / len(shards))
        return jnp.repeat(jnp.exp(heights), dims[axis_at] // blocks).reshape((-1,) + (1,) * (len(dims) - axis_at - 1))

    loudness = one(*shards[0])
    for cut in shards[1:]:
        loudness = loudness * one(*cut)
    return loudness


def normal_values(stream_key, dims, width, bound, cuts=(), kind=jnp.bfloat16):
    drawn = jax.random.normal(stream_key, dims, jnp.float32) * width
    if len(cuts) > 0:
        drawn = level_of(stream_key, dims, cuts, -0.22, 0.18) * drawn
    return jnp.clip(drawn, min=-bound, max=bound).astype(kind)


def setup_inputs(seed: int = 0) -> dict:
    keys = jax.random.split(jax.random.key(seed), 11)
    return {
        "position": normal_values(keys[0], (3, PARTICLES), 1.0, 6.0, ((1, 32),), jnp.float32),
        "particle_mass": jnp.clip(jnp.exp(math.log(2.0) - 1.3862944 * jax.random.uniform(keys[1], (PARTICLES,), jnp.float32) ** level_of(keys[1], (PARTICLES,), ((0, 32),), -0.2, 0.2)), 0.5, 2.0),
        "settling": jnp.clip(jnp.exp(math.log(1.0) - 2.9957323 * jax.random.uniform(keys[2], (PARTICLES,), jnp.float32) ** level_of(keys[2], (PARTICLES,), ((0, 32),), -0.2, 0.2)), 0.05, 1.0),
        "walk_noise": normal_values(keys[3], (STEPS, 3, PARTICLES), 1.0, 6.0, ((2, 32),), jnp.float32),
        "velocity": normal_values(keys[4], (SLABS, 3, NT, CELLS), 1.0, 6.0, ((2, 32),)),
        "diffusivity": jnp.clip(jnp.exp(math.log(0.5) - 3.224016 * jax.random.uniform(keys[5], (SLABS, NT, CELLS), jnp.float32) ** level_of(keys[5], (SLABS, NT, CELLS), ((1, 32),), -0.2, 0.2)), 0.019897461, 0.5).astype(jnp.bfloat16),
        "block_tile": draw_block_tile(jax.random.fold_in(keys[10], 71), 0),
        "cell_index": touch_ends(jax.random.randint(keys[7], (STEPS, PARTICLES), 0, CELLS), jax.random.fold_in(keys[7], 1), 0, CELLS - 1).astype(jnp.int32),
        "bed_cell": touch_ends(jax.random.randint(keys[8], (STEPS, PARTICLES), 0, BEDC), jax.random.fold_in(keys[8], 1), 0, BEDC - 1).astype(jnp.int32),
        "route_code": jax.vmap(lambda own: jax.random.permutation(own, NB))(jax.random.split(keys[9], (STEPS - 1) * DEVICES)).reshape((STEPS - 1, DEVICES, NB)).astype(jnp.int32),
    }


time_step = 0.5

def reference(position, particle_mass, settling, walk_noise, velocity, diffusivity, block_tile, cell_index, bed_cell, route_code):
    bed_total = jnp.zeros((NT * BEDC,), jnp.float32)
    places = position
    masses = particle_mass
    speeds = settling
    device_ids = jnp.arange(DEVICES, dtype=jnp.int32)
    arch_ids = device_ids // N_DOM
    dom_ids = device_ids % N_DOM
    for step in range(STEPS):
        tiles = jnp.repeat(block_tile[step].reshape(-1), BLOCK).astype(jnp.int32)
        cells = cell_index[step]
        first_vel = velocity[step][:, tiles, cells].astype(jnp.float32)
        second_vel = velocity[step + 1][:, tiles, cells].astype(jnp.float32)
        first_diff = diffusivity[step][tiles, cells].astype(jnp.float32)
        second_diff = diffusivity[step + 1][tiles, cells].astype(jnp.float32)
        drift = 0.5 * time_step * (first_vel + second_vel)
        drift = drift.at[2].add(-time_step * speeds)
        places = places + drift + jnp.sqrt(time_step * (first_diff + second_diff)) * walk_noise[step]
        deposit = masses * (1.0 - jnp.exp(-time_step * speeds))
        masses = masses - deposit
        bins = (tiles * BEDC + bed_cell[step]).astype(jnp.int32)
        bed_total = bed_total.at[bins].add(deposit)
        if step + 1 < STEPS:
            codes = route_code[step]
            peers = codes // BLK_PEER
            within = codes % BLK_PEER
            target = ((arch_ids[:, None] * N_DOM + peers) * NB + dom_ids[:, None] * BLK_PEER + within).reshape(-1).astype(jnp.int32)
            place_blocks = places.reshape(3, DEVICES * NB, BLOCK)
            places = jnp.zeros_like(place_blocks).at[:, target].set(place_blocks).reshape(3, -1)
            mass_blocks = masses.reshape(DEVICES * NB, BLOCK)
            masses = jnp.zeros_like(mass_blocks).at[target].set(mass_blocks).reshape(-1)
            speed_blocks = speeds.reshape(DEVICES * NB, BLOCK)
            speeds = jnp.zeros_like(speed_blocks).at[target].set(speed_blocks).reshape(-1)
    scale_factor = TILE_ARCH * BEDC / PART_DEV
    return (places, masses, (bed_total * scale_factor).reshape(NT, BEDC))
```

```python
import functools
import math

import jax
import jax.numpy as jnp
from jax import lax
from jax.experimental import pallas as pl
from jax.experimental.pallas import tpu as pltpu
from jax.sharding import PartitionSpec as P

MESH = pl.DeviceIdType.MESH
BF16 = jnp.bfloat16
F32 = jnp.float32

BEDC = 512
LANES = 128
time_step = 0.5


def kernel(
    doms, archs, nblocks, width, steps, slabs, rows, scale,
    pos_hbm, mass_hbm, settle_hbm, noise_hbm, vel_hbm, diff_hbm, tile_hbm, cell_hbm, bed_hbm, route_hbm,
    pos_out, mass_out, bed_out,
    pos, mass, settle, noise, vel, diff, tile, cell, bed, route,
    spread_rows, table, inverse, decay, dep, delta,
    carried_send, carried_recv, pos_send, pos_recv,
    bed_part, bed_recv,
    in_sem, table_sem, carried_sem, pos_sem, bed_sem,
):
    me = lax.axis_index("dom")
    arch = lax.axis_index("arch")
    twin = lax.rem(arch + 1, archs)
    group = math.gcd(nblocks, 8)

    barrier = pltpu.get_barrier_semaphore()

    def greet(p, _):
        pl.semaphore_signal(barrier, inc=1, device_id={"dom": lax.rem(me + p, doms)}, device_id_type=MESH)
        return 0

    lax.fori_loop(1, doms, greet, 0)
    pl.semaphore_signal(barrier, inc=1, device_id={"arch": twin}, device_id_type=MESH)

    staged = [
        pltpu.make_async_copy(src, dst, in_sem.at[i])
        for i, (src, dst) in enumerate(
            [
                (tile_hbm, tile), (route_hbm, route), (vel_hbm, vel), (diff_hbm, diff), (mass_hbm, mass),
                (settle_hbm, settle), (bed_hbm, bed), (cell_hbm, cell), (pos_hbm, pos), (noise_hbm, noise),
            ]
        )
    ]
    for copy in staged:
        copy.start()
    for copy in staged[:2]:
        copy.wait()

    for step in range(steps - 1):
        def invert(c, _, step=step):
            def probe(j, found):
                return jnp.where(route[step, 0, j] == c, j, found)

            inverse[step, c] = lax.fori_loop(0, nblocks, probe, jnp.int32(0), unroll=True if nblocks <= 16 else 16)
            return 0

        lax.fori_loop(0, nblocks, invert, 0)

    for copy in staged[2:4]:
        copy.wait()
    for ch in range(4):
        raw = (vel[ch] if ch < 3 else diff[...]).astype(F32)
        for r in range(rows):
            spread_rows[ch, pl.ds(r, slabs, stride=rows), :] = raw[:, r * LANES : (r + 1) * LANES]
    for slab in range(slabs):
        for ch in range(4):
            table[arch, slab, ch] = spread_rows[ch, slab * rows : (slab + 1) * rows, :].astype(BF16)

    for copy in staged[4:7]:
        copy.wait()
    fade = jnp.exp(-time_step * settle[...])
    decay[...] = fade
    dep[...] = mass[...] * (1.0 - fade)
    mass[...] = mass[...] * fade

    pl.semaphore_wait(barrier, doms - 1 + archs - 1)

    table_copy = pltpu.make_async_remote_copy(
        src_ref=table.at[arch], dst_ref=table.at[arch], send_sem=table_sem.at[0], recv_sem=table_sem.at[1],
        device_id={"arch": twin}, device_id_type=MESH,
    )
    table_copy.start()

    def send(step, sbuf, rbuf, sem, p):
        pltpu.make_async_remote_copy(
            src_ref=sbuf[step].at[p], dst_ref=rbuf[step].at[me], send_sem=sem.at[step, 0], recv_sem=sem.at[step, 1],
            device_id={"dom": lax.rem(me + p, doms)}, device_id_type=MESH,
        ).start()

    def whole(step, sbuf, rbuf, sem):
        return pltpu.make_async_remote_copy(
            src_ref=sbuf[step].at[pl.ds(1, doms - 1)], dst_ref=rbuf[step].at[pl.ds(1, doms - 1)],
            send_sem=sem.at[step, 0], recv_sem=sem.at[step, 1],
            device_id={"dom": lax.rem(me + 1, doms)}, device_id_type=MESH,
        )

    def send_carried(step, source):
        def load(p):
            return source(inverse[step, lax.rem(me + p, doms)])

        m, e = load(0)
        carried_recv[step][me, 0:2, :] = m
        carried_recv[step][me, 2:4, :] = e

        def one(p, _):
            m, e = load(p)
            carried_send[step][p, 0:2, :] = m
            carried_send[step][p, 2:4, :] = e
            send(step, carried_send, carried_recv, carried_sem, p)
            return 0

        lax.fori_loop(1, doms, one, 0, unroll=5 if doms == 16 else 1)

    send_carried(0, lambda j: (mass[j], decay[j]))

    def deposits(step, total):
        bed_ids = lax.broadcasted_iota(jnp.int32, (LANES, width), 0)
        row_ids = lax.broadcasted_iota(jnp.int32, (8, width), 0)

        def several(k, total):
            weights, hits = [], []
            for i in range(group):
                j = k * group + i
                cells = bed[step : step + 1, pl.ds(pl.multiple_of(j * width, width), width)]
                local = lax.div(tile[step, 0, j], doms)
                home = local * (BEDC // LANES) + cells // LANES
                amount = jnp.concatenate([dep[j, 0:1, :], dep[j, 1:2, :]], axis=1)
                weight = jnp.where(home == row_ids, amount, 0.0)
                high = weight.astype(BF16)
                low = (weight - high.astype(F32)).astype(BF16)
                weights.append(jnp.concatenate([high, low], axis=0))
                hits.append(jnp.where(cells % LANES == bed_ids, 1.0, 0.0).astype(BF16))
            return total + lax.dot_general(
                jnp.concatenate(weights, axis=1), jnp.concatenate(hits, axis=1),
                (((1,), (1,)), ((), ())), preferred_element_type=F32,
            )

        return lax.fori_loop(0, nblocks // group, several, total)

    channel_ids = lax.broadcasted_iota(jnp.int32, (16, 2 * 4 * rows), 1) // rows % 4
    out_ids = lax.broadcasted_iota(jnp.int32, (16, 2 * 4 * rows), 0)
    mix = jnp.where(
        out_ids < 8,
        jnp.where(channel_ids == out_ids, 0.5 * time_step, 0.0),
        jnp.where(channel_ids == 3, time_step, 0.0),
    ).astype(BF16)
    lane_ids = lax.broadcasted_iota(jnp.int32, (LANES, width), 0)
    cell_rows = lax.broadcasted_iota(jnp.int32, (rows, width), 0)

    def walk(step, blocks):
        picked = []
        for j in blocks:
            cells = cell[step : step + 1, pl.ds(pl.multiple_of(j * width, width), width)]
            column_hit = jnp.where(cells % LANES == lane_ids, 1.0, 0.0).astype(BF16)
            row_hit = jnp.where(cells // LANES == cell_rows, 1.0, 0.0).astype(BF16)
            local = lax.div(tile[step, 0, j], doms)
            both = jnp.concatenate(
                [table[local, slab].reshape(4 * rows, LANES) for slab in (step, step + 1)], axis=0
            )
            found = jnp.dot(both, column_hit, preferred_element_type=F32).astype(BF16)
            found = found.reshape(8, rows, width) * row_hit[None]
            picked.append(found.reshape(8 * rows, width))
        mixed = jnp.dot(mix, jnp.concatenate(picked, axis=1), preferred_element_type=F32)
        moves = []
        for i, j in enumerate(blocks):
            part = mixed[:, i * width : (i + 1) * width]
            draw = noise[step, :, pl.ds(pl.multiple_of(j * width, width), width)]
            moves.append(part[0:3] + jnp.sqrt(part[8:11]) * draw)
        return moves

    third = (lax.broadcasted_iota(jnp.int32, (3, width), 0) == 2)

    for copy in staged[7:]:
        copy.wait()
    table_copy.wait_recv()

    def first(k, _):
        blocks = [k * group + i for i in range(group)]
        moves = walk(0, blocks)
        values = []
        for j, move in zip(blocks, moves):
            speed = jnp.concatenate([settle[j, 0:1, :], settle[j, 1:2, :]], axis=1)
            sink = jnp.where(third, steps * time_step * speed, 0.0)
            here = pos[:, pl.ds(pl.multiple_of(j * width, width), width)]
            values.append(here - sink + move)
        for j, value in zip(blocks, values):
            delta[j] = value
        return 0

    lax.fori_loop(0, nblocks // group, first, 0)

    def send_places(step, source):
        def one(p, _):
            pos_send[step][p] = source(inverse[step, lax.rem(me + p, doms)])
            send(step, pos_send, pos_recv, pos_sem, p)
            return 0

        lax.fori_loop(1, doms, one, 0, unroll=5 if doms == 16 else 1)
        pos_recv[step][me] = source(inverse[step, me])

    send_places(0, lambda j: delta[j])

    total = deposits(0, jnp.zeros((16, LANES), F32))

    def rest(step):
        def some(k, _):
            moves = walk(step, [k * group + i for i in range(group)])
            for i, move in enumerate(moves):
                delta[k * group + i] = move
            return 0

        lax.fori_loop(0, nblocks // group, some, 0)

    for step in range(1, steps):
        whole(step - 1, carried_send, carried_recv, carried_sem).wait_recv()
        masses = carried_recv[step - 1][:, 0:2, :]
        fade = carried_recv[step - 1][:, 2:4, :]
        left = masses * fade
        dep[...] = masses - left
        if step + 1 < steps:
            def source(j, step=step):
                fade = carried_recv[step - 1][j, 2:4, :]
                return carried_recv[step - 1][j, 0:2, :] * fade, fade

            send_carried(step, source)
        else:
            mass_out[...] = left
        rest(step)
        if step + 1 == steps:
            total = deposits(step, total)
            for t in range(archs):
                q = BEDC // LANES
                bed_part[t] = (total[t * q : (t + 1) * q] + total[8 + t * q : 8 + (t + 1) * q]) * scale
            bed_copy = pltpu.make_async_remote_copy(
                src_ref=bed_part.at[twin], dst_ref=bed_recv, send_sem=bed_sem.at[0], recv_sem=bed_sem.at[1],
                device_id={"arch": twin}, device_id_type=MESH,
            )
            bed_copy.start()
        whole(step - 1, pos_send, pos_recv, pos_sem).wait_recv()
        if step + 1 < steps:
            send_places(step, lambda j, step=step: pos_recv[step - 1][j] + delta[j])
            total = deposits(step, total)

    last = steps - 2
    def finish(j, _):
        pos_out[:, pl.ds(pl.multiple_of(j * width, width), width)] = pos_recv[last][j] + delta[j]
        return 0

    lax.fori_loop(0, nblocks, finish, 0, unroll=16)
    bed_copy.wait_recv()
    bed_out[...] = bed_part[arch] + bed_recv[...]

    table_copy.wait_send()
    bed_copy.wait_send()
    for step in range(steps - 1):
        whole(step, carried_send, carried_recv, carried_sem).wait_send()
        whole(step, pos_send, pos_recv, pos_sem).wait_send()


def body(
    position, particle_mass, settling, walk_noise, velocity, diffusivity, block_tile, cell_index, bed_cell, route_code
):
    doms = lax.axis_size("dom")
    archs = lax.axis_size("arch")
    particles = position.shape[1]
    nblocks = block_tile.shape[2]
    width = particles // nblocks
    steps = cell_index.shape[0]
    slabs, _, _, cells = velocity.shape
    rows = cells // LANES
    half = width // LANES
    moves = steps - 1
    in_hbm = pl.BlockSpec(memory_space=pltpu.HBM)
    in_vmem = pl.BlockSpec(memory_space=pltpu.VMEM)
    vmem = pltpu.VMEM
    args = (
        position,
        particle_mass.reshape(nblocks, half, LANES),
        settling.reshape(nblocks, half, LANES),
        walk_noise,
        velocity.transpose(1, 2, 0, 3).reshape(3, slabs, cells),
        diffusivity.transpose(1, 0, 2).reshape(slabs, cells),
        block_tile,
        cell_index,
        bed_cell,
        route_code,
    )
    places, masses, beds = pl.pallas_call(
        functools.partial(
            kernel, doms, archs, nblocks, width, steps, slabs, rows, BEDC / particles
        ),
        out_shape=(
            jax.ShapeDtypeStruct((3, particles), F32),
            jax.ShapeDtypeStruct((nblocks, half, LANES), F32),
            jax.ShapeDtypeStruct((BEDC // LANES, LANES), F32),
        ),
        in_specs=[in_hbm] * len(args),
        out_specs=(in_vmem, in_vmem, in_vmem),
        scratch_shapes=[
            vmem(args[0].shape, F32),
            vmem(args[1].shape, F32),
            vmem(args[2].shape, F32),
            vmem(args[3].shape, F32),
            vmem(args[4].shape, BF16),
            vmem(args[5].shape, BF16),
            pltpu.SMEM(args[6].shape, jnp.int32),
            vmem(args[7].shape, jnp.int32),
            vmem(args[8].shape, jnp.int32),
            pltpu.SMEM(args[9].shape, jnp.int32),
            vmem((4, slabs * rows, LANES), F32),
            vmem((archs, slabs, 4, rows, LANES), BF16),
            pltpu.SMEM((moves, nblocks), jnp.int32),
            vmem((nblocks, half, LANES), F32),
            vmem((nblocks, half, LANES), F32),
            vmem((nblocks, 3, width), F32),
            [vmem((nblocks, 2 * half, LANES), F32)] * moves,
            [vmem((nblocks, 2 * half, LANES), F32)] * moves,
            [vmem((nblocks, 3, width), F32)] * moves,
            [vmem((nblocks, 3, width), F32)] * moves,
            vmem((archs, BEDC // LANES, LANES), F32),
            vmem((BEDC // LANES, LANES), F32),
            pltpu.SemaphoreType.DMA((len(args),)),
            pltpu.SemaphoreType.DMA((2,)),
            pltpu.SemaphoreType.DMA((moves, 2)),
            pltpu.SemaphoreType.DMA((moves, 2)),
            pltpu.SemaphoreType.DMA((2,)),
        ],
        compiler_params=pltpu.CompilerParams(
            collective_id=0, has_side_effects=True, vmem_limit_bytes=60 * 1024 * 1024
        ),
    )(*args)
    return places, masses.reshape(particles), beds.reshape(1, BEDC)


def solution(mesh):
    return jax.shard_map(
        body,
        mesh=mesh,
        in_specs=(
            P(None, ("arch", "dom")),
            P(("arch", "dom")),
            P(("arch", "dom")),
            P(None, None, ("arch", "dom")),
            P(None, None, ("arch", "dom"), None),
            P(None, ("arch", "dom"), None),
            P(None, ("arch", "dom"), None),
            P(None, ("arch", "dom")),
            P(None, ("arch", "dom")),
            P(None, ("arch", "dom"), None),
        ),
        out_specs=(P(None, ("arch", "dom")), P(("arch", "dom")), P(("arch", "dom"), None)),
        check_vma=False,
    )
```

```python
import functools
import math

import jax
import jax.numpy as jnp
from jax import lax
from jax.experimental import pallas as pl
from jax.experimental.pallas import tpu as pltpu
from jax.sharding import PartitionSpec as P

MESH = pl.DeviceIdType.MESH
BF16 = jnp.bfloat16
F32 = jnp.float32

BEDC = 512
LANES = 128
time_step = 0.5


def kernel(
    doms, archs, nblocks, width, steps, slabs, rows, scale,
    pos_hbm, mass_hbm, settle_hbm, noise_hbm, vel_hbm, diff_hbm, tile_hbm, cell_hbm, bed_hbm, route_hbm,
    pos_out, mass_out, bed_out,
    pos, mass, settle, noise, vel, diff, tile, cell, bed, route,
    spread_rows, table, inverse, decay, dep, delta,
    carried_send, carried_recv, pos_send, pos_recv,
    bed_part, bed_recv,
    in_sem, table_sem, carried_sem, pos_sem, bed_sem,
):
    me = lax.axis_index("dom")
    arch = lax.axis_index("arch")
    twin = lax.rem(arch + 1, archs)
    group = math.gcd(nblocks, 8)

    staged = [
        pltpu.make_async_copy(src, dst, in_sem.at[i])
        for i, (src, dst) in enumerate(
            [
                (vel_hbm, vel), (diff_hbm, diff), (tile_hbm, tile), (route_hbm, route), (mass_hbm, mass),
                (settle_hbm, settle), (bed_hbm, bed), (cell_hbm, cell), (pos_hbm, pos), (noise_hbm, noise),
            ]
        )
    ]
    for copy in staged[:2]:
        copy.start()

    barrier = pltpu.get_barrier_semaphore()

    def greet(p, _):
        pl.semaphore_signal(barrier, inc=1, device_id={"dom": lax.rem(me + p, doms)}, device_id_type=MESH)
        return 0

    lax.fori_loop(1, doms, greet, 0)
    pl.semaphore_signal(barrier, inc=1, device_id={"arch": twin}, device_id_type=MESH)

    for copy in staged[2:]:
        copy.start()

    def find_inverse(step):
        def invert(c, _):
            def probe(j, found):
                return jnp.where(route[step, 0, j] == c, j, found)

            inverse[step, c] = lax.fori_loop(0, nblocks, probe, jnp.int32(0), unroll=True if nblocks <= 16 else 16)
            return 0

        lax.fori_loop(0, nblocks, invert, 0, unroll=4)

    for copy in staged[:2]:
        copy.wait()
    for ch in range(4):
        raw = (vel[ch] if ch < 3 else diff[...]).astype(F32)
        for r in range(rows):
            spread_rows[ch, pl.ds(r, slabs, stride=rows), :] = raw[:, r * LANES : (r + 1) * LANES]
    for slab in range(slabs):
        for ch in range(4):
            table[arch, slab, ch] = spread_rows[ch, slab * rows : (slab + 1) * rows, :].astype(BF16)

    pl.semaphore_wait(barrier, doms - 1 + archs - 1)

    table_copy = pltpu.make_async_remote_copy(
        src_ref=table.at[arch], dst_ref=table.at[arch], send_sem=table_sem.at[0], recv_sem=table_sem.at[1],
        device_id={"arch": twin}, device_id_type=MESH,
    )
    table_copy.start()

    for copy in staged[2:7]:
        copy.wait()
    fade = jnp.exp(-time_step * settle[...])
    decay[...] = fade
    dep[...] = mass[...] * (1.0 - fade)
    mass[...] = mass[...] * fade
    find_inverse(0)

    def send(step, sbuf, rbuf, sem, p):
        pltpu.make_async_remote_copy(
            src_ref=sbuf[step].at[p], dst_ref=rbuf[step].at[me], send_sem=sem.at[step, 0], recv_sem=sem.at[step, 1],
            device_id={"dom": lax.rem(me + p, doms)}, device_id_type=MESH,
        ).start()

    def whole(step, sbuf, rbuf, sem):
        return pltpu.make_async_remote_copy(
            src_ref=sbuf[step].at[pl.ds(1, doms - 1)], dst_ref=rbuf[step].at[pl.ds(1, doms - 1)],
            send_sem=sem.at[step, 0], recv_sem=sem.at[step, 1],
            device_id={"dom": lax.rem(me + 1, doms)}, device_id_type=MESH,
        )

    def send_carried(step, source):
        def load(p):
            return source(inverse[step, lax.rem(me + p, doms)])

        m, e = load(0)
        carried_recv[step][me, 0:2, :] = m
        carried_recv[step][me, 2:4, :] = e

        def one(p, _):
            m, e = load(p)
            carried_send[step][p, 0:2, :] = m
            carried_send[step][p, 2:4, :] = e
            send(step, carried_send, carried_recv, carried_sem, p)
            return 0

        lax.fori_loop(1, doms, one, 0, unroll=5 if doms == 16 else 1)

    send_carried(0, lambda j: (mass[j], decay[j]))

    tall_ids = lax.broadcasted_iota(jnp.int32, (LANES, width), 0).astype(BF16)
    cell_rows = lax.broadcasted_iota(jnp.int32, (rows, width), 0)
    home_rows = lax.broadcasted_iota(jnp.int32, (8, width), 0)

    def low_hits(cells):
        low = jnp.broadcast_to(lax.bitwise_and(cells, LANES - 1), (16, width)).astype(BF16)
        low = jnp.broadcast_to(low[None], (LANES // 16, 16, width)).reshape(LANES, width)
        return jnp.where(low == tall_ids, jnp.ones((), BF16), jnp.zeros((), BF16))

    def high_bits(cells):
        return lax.shift_right_logical(cells, 7)

    def deposits(step, blocks):
        weights, hits = [], []
        for j in blocks:
            cells = bed[step : step + 1, pl.ds(pl.multiple_of(j * width, width), width)]
            local = lax.div(tile[step, 0, j], doms)
            home = local * (BEDC // LANES) + high_bits(cells)
            amount = jnp.concatenate([dep[j, 0:1, :], dep[j, 1:2, :]], axis=1)
            weight = jnp.where(home == home_rows, amount, 0.0)
            high = weight.astype(BF16)
            low = (weight - high.astype(F32)).astype(BF16)
            weights.append(jnp.concatenate([high, low], axis=0))
            hits.append(low_hits(cells))
        return lax.dot_general(
            jnp.concatenate(weights, axis=1), jnp.concatenate(hits, axis=1),
            (((1,), (1,)), ((), ())), preferred_element_type=F32,
        )

    def all_deposits(step, total):
        def some(k, total):
            return total + deposits(step, [k * group + i for i in range(group)])

        return lax.fori_loop(0, nblocks // group, some, total)

    channel_ids = lax.broadcasted_iota(jnp.int32, (16, 2 * 4 * rows), 1) // rows % 4
    out_ids = lax.broadcasted_iota(jnp.int32, (16, 2 * 4 * rows), 0)
    mix = jnp.where(
        out_ids < 8,
        jnp.where(channel_ids == out_ids, 0.5 * time_step, 0.0),
        jnp.where(channel_ids == 3, time_step, 0.0),
    ).astype(BF16)

    def walk(step, blocks):
        picked = []
        for j in blocks:
            cells = cell[step : step + 1, pl.ds(pl.multiple_of(j * width, width), width)]
            row_hit = jnp.where(high_bits(cells) == cell_rows, 1.0, 0.0).astype(BF16)
            local = lax.div(tile[step, 0, j], doms)
            both = jnp.concatenate(
                [table[local, slab].reshape(4 * rows, LANES) for slab in (step, step + 1)], axis=0
            )
            found = jnp.dot(both, low_hits(cells), preferred_element_type=F32).astype(BF16)
            found = found.reshape(8, rows, width) * row_hit[None]
            picked.append(found.reshape(8 * rows, width))
        mixed = jnp.dot(mix, jnp.concatenate(picked, axis=1), preferred_element_type=F32)
        moves = []
        for i, j in enumerate(blocks):
            part = mixed[:, i * width : (i + 1) * width]
            draw = noise[step, :, pl.ds(pl.multiple_of(j * width, width), width)]
            moves.append(part[0:3] + jnp.sqrt(part[8:11]) * draw)
        return moves

    third = (lax.broadcasted_iota(jnp.int32, (3, width), 0) == 2)

    total = all_deposits(0, jnp.zeros((16, LANES), F32))

    for copy in staged[7:]:
        copy.wait()
    table_copy.wait_recv()

    def first(k, _):
        blocks = [k * group + i for i in range(group)]
        moves = walk(0, blocks)
        values = []
        for j, move in zip(blocks, moves):
            speed = jnp.concatenate([settle[j, 0:1, :], settle[j, 1:2, :]], axis=1)
            sink = jnp.where(third, steps * time_step * speed, 0.0)
            here = pos[:, pl.ds(pl.multiple_of(j * width, width), width)]
            values.append(here - sink + move)
        for j, value in zip(blocks, values):
            delta[j] = value
        return 0

    lax.fori_loop(0, nblocks // group, first, 0)

    def send_places(step, source):
        def one(p, _):
            pos_send[step][p] = source(inverse[step, lax.rem(me + p, doms)])
            send(step, pos_send, pos_recv, pos_sem, p)
            return 0

        lax.fori_loop(1, doms, one, 0, unroll=5 if doms == 16 else 1)
        pos_recv[step][me] = source(inverse[step, me])

    send_places(0, lambda j: delta[j])

    for step in range(1, steps):
        if step + 1 < steps:
            find_inverse(step)
        whole(step - 1, carried_send, carried_recv, carried_sem).wait_recv()
        masses = carried_recv[step - 1][:, 0:2, :]
        fade = carried_recv[step - 1][:, 2:4, :]
        left = masses * fade
        dep[...] = masses - left
        if step + 1 < steps:
            def source(j, step=step):
                fade = carried_recv[step - 1][j, 2:4, :]
                return carried_recv[step - 1][j, 0:2, :] * fade, fade

            send_carried(step, source)
        else:
            mass_out[...] = left

        def some(k, total, step=step):
            blocks = [k * group + i for i in range(group)]
            moves = walk(step, blocks)
            total = total + deposits(step, blocks)
            for j, move in zip(blocks, moves):
                delta[j] = move
            return total

        total = lax.fori_loop(0, nblocks // group, some, total)
        if step + 1 == steps:
            for t in range(archs):
                q = BEDC // LANES
                bed_part[t] = (total[t * q : (t + 1) * q] + total[8 + t * q : 8 + (t + 1) * q]) * scale
            bed_copy = pltpu.make_async_remote_copy(
                src_ref=bed_part.at[twin], dst_ref=bed_recv, send_sem=bed_sem.at[0], recv_sem=bed_sem.at[1],
                device_id={"arch": twin}, device_id_type=MESH,
            )
            bed_copy.start()
        whole(step - 1, pos_send, pos_recv, pos_sem).wait_recv()
        if step + 1 < steps:
            send_places(step, lambda j, step=step: pos_recv[step - 1][j] + delta[j])

    last = steps - 2
    def finish(j, _):
        pos_out[:, pl.ds(pl.multiple_of(j * width, width), width)] = pos_recv[last][j] + delta[j]
        return 0

    lax.fori_loop(0, nblocks, finish, 0, unroll=16)
    bed_copy.wait_recv()
    bed_out[...] = bed_part[arch] + bed_recv[...]

    table_copy.wait_send()
    bed_copy.wait_send()
    for step in range(steps - 1):
        whole(step, carried_send, carried_recv, carried_sem).wait_send()
        whole(step, pos_send, pos_recv, pos_sem).wait_send()


def write_out(*refs):
    count = len(refs) // 2
    sem = refs[-1]
    copies = [pltpu.make_async_copy(refs[i], refs[count + i], sem.at[i]) for i in range(count)]
    for copy in copies:
        copy.start()
    for copy in copies:
        copy.wait()


def body(
    position, particle_mass, settling, walk_noise, velocity, diffusivity, block_tile, cell_index, bed_cell, route_code
):
    doms = lax.axis_size("dom")
    archs = lax.axis_size("arch")
    particles = position.shape[1]
    nblocks = block_tile.shape[2]
    width = particles // nblocks
    steps = cell_index.shape[0]
    slabs, _, _, cells = velocity.shape
    rows = cells // LANES
    half = width // LANES
    moves = steps - 1
    in_hbm = pl.BlockSpec(memory_space=pltpu.HBM)
    in_vmem = pl.BlockSpec(memory_space=pltpu.VMEM)
    vmem = pltpu.VMEM
    args = (
        position,
        particle_mass.reshape(nblocks, half, LANES),
        settling.reshape(nblocks, half, LANES),
        walk_noise,
        velocity.transpose(1, 2, 0, 3).reshape(3, slabs, cells),
        diffusivity.transpose(1, 0, 2).reshape(slabs, cells),
        block_tile,
        cell_index,
        bed_cell,
        route_code,
    )
    results = pl.pallas_call(
        functools.partial(
            kernel, doms, archs, nblocks, width, steps, slabs, rows, BEDC / particles
        ),
        out_shape=(
            pltpu.VMEM((3, particles), F32),
            pltpu.VMEM((nblocks, half, LANES), F32),
            pltpu.VMEM((BEDC // LANES, LANES), F32),
        ),
        in_specs=[in_hbm] * len(args),
        out_specs=(in_vmem, in_vmem, in_vmem),
        scratch_shapes=[
            vmem(args[0].shape, F32),
            vmem(args[1].shape, F32),
            vmem(args[2].shape, F32),
            vmem(args[3].shape, F32),
            vmem(args[4].shape, BF16),
            vmem(args[5].shape, BF16),
            pltpu.SMEM(args[6].shape, jnp.int32),
            vmem(args[7].shape, jnp.int32),
            vmem(args[8].shape, jnp.int32),
            pltpu.SMEM(args[9].shape, jnp.int32),
            vmem((4, slabs * rows, LANES), F32),
            vmem((archs, slabs, 4, rows, LANES), BF16),
            pltpu.SMEM((moves, nblocks), jnp.int32),
            vmem((nblocks, half, LANES), F32),
            vmem((nblocks, half, LANES), F32),
            vmem((nblocks, 3, width), F32),
            [vmem((nblocks, 2 * half, LANES), F32)] * moves,
            [vmem((nblocks, 2 * half, LANES), F32)] * moves,
            [vmem((nblocks, 3, width), F32)] * moves,
            [vmem((nblocks, 3, width), F32)] * moves,
            vmem((archs, BEDC // LANES, LANES), F32),
            vmem((BEDC // LANES, LANES), F32),
            pltpu.SemaphoreType.DMA((len(args),)),
            pltpu.SemaphoreType.DMA((2,)),
            pltpu.SemaphoreType.DMA((moves, 2)),
            pltpu.SemaphoreType.DMA((moves, 2)),
            pltpu.SemaphoreType.DMA((2,)),
        ],
        compiler_params=pltpu.CompilerParams(
            collective_id=0, has_side_effects=True, vmem_limit_bytes=60 * 1024 * 1024
        ),
    )(*args)
    places, masses, beds = pl.pallas_call(
        write_out,
        out_shape=tuple(jax.ShapeDtypeStruct(r.shape, F32) for r in results),
        in_specs=[in_vmem] * 3,
        out_specs=(in_hbm,) * 3,
        scratch_shapes=[pltpu.SemaphoreType.DMA((3,))],
    )(*results)
    return places, masses.reshape(particles), beds.reshape(1, BEDC)


def solution(mesh):
    return jax.shard_map(
        body,
        mesh=mesh,
        in_specs=(
            P(None, ("arch", "dom")),
            P(("arch", "dom")),
            P(("arch", "dom")),
            P(None, None, ("arch", "dom")),
            P(None, None, ("arch", "dom"), None),
            P(None, ("arch", "dom"), None),
            P(None, ("arch", "dom"), None),
            P(None, ("arch", "dom")),
            P(None, ("arch", "dom")),
            P(None, ("arch", "dom"), None),
        ),
        out_specs=(P(None, ("arch", "dom")), P(("arch", "dom")), P(("arch", "dom"), None)),
        check_vma=False,
    )
```

```python
import functools
import math

import jax
import jax.numpy as jnp
from jax import lax
from jax.experimental import pallas as pl
from jax.experimental.pallas import tpu as pltpu
from jax.sharding import PartitionSpec as P

MESH = pl.DeviceIdType.MESH
BF16 = jnp.bfloat16
F32 = jnp.float32

BEDC = 512
LANES = 128
time_step = 0.5


def kernel(
    doms, archs, nblocks, width, steps, slabs, rows, scale,
    pos_hbm, mass_hbm, settle_hbm, noise_hbm, vel_hbm, diff_hbm, tile_hbm, cell_hbm, bed_hbm, route_hbm,
    pos_out, mass_out, bed_out,
    pos, mass, settle, noise, vel, diff, tile, cell, bed, route,
    spread_rows, table, inverse, decay, dep, delta,
    carried_send, carried_recv, pos_send, pos_recv,
    bed_part, bed_recv,
    in_sem, table_sem, carried_sem, pos_sem, bed_sem,
):
    me = lax.axis_index("dom")
    arch = lax.axis_index("arch")
    twin = lax.rem(arch + 1, archs)
    group = math.gcd(nblocks, 16)

    staged = [
        pltpu.make_async_copy(src, dst, in_sem.at[i])
        for i, (src, dst) in enumerate(
            [
                (vel_hbm, vel), (diff_hbm, diff), (tile_hbm, tile), (route_hbm, route), (mass_hbm, mass),
                (settle_hbm, settle), (bed_hbm, bed), (cell_hbm, cell), (pos_hbm, pos), (noise_hbm, noise),
            ]
        )
    ]
    for copy in staged[:2]:
        copy.start()

    barrier = pltpu.get_barrier_semaphore()

    def greet(p, _):
        pl.semaphore_signal(barrier, inc=1, device_id={"dom": lax.rem(me + p, doms)}, device_id_type=MESH)
        return 0

    lax.fori_loop(1, doms, greet, 0)
    pl.semaphore_signal(barrier, inc=1, device_id={"arch": twin}, device_id_type=MESH)

    for copy in staged[2:]:
        copy.start()

    def find_inverse(step):
        def invert(c, _):
            def probe(j, found):
                return jnp.where(route[step, 0, j] == c, j, found)

            inverse[step, c] = lax.fori_loop(0, nblocks, probe, jnp.int32(0), unroll=True if nblocks <= 16 else 16)
            return 0

        lax.fori_loop(0, nblocks, invert, 0, unroll=4)

    for copy in staged[:2]:
        copy.wait()
    for ch in range(4):
        raw = (vel[ch] if ch < 3 else diff[...]).astype(F32)
        for r in range(rows):
            spread_rows[ch, pl.ds(r, slabs, stride=rows), :] = raw[:, r * LANES : (r + 1) * LANES]
    for slab in range(slabs):
        for ch in range(4):
            table[arch, slab, ch] = spread_rows[ch, slab * rows : (slab + 1) * rows, :].astype(BF16)

    pl.semaphore_wait(barrier, doms - 1 + archs - 1)

    table_copy = pltpu.make_async_remote_copy(
        src_ref=table.at[arch], dst_ref=table.at[arch], send_sem=table_sem.at[0], recv_sem=table_sem.at[1],
        device_id={"arch": twin}, device_id_type=MESH,
    )
    table_copy.start()

    for copy in staged[2:7]:
        copy.wait()
    fade = jnp.exp(-time_step * settle[...])
    decay[...] = fade
    dep[...] = mass[...] * (1.0 - fade)
    mass[...] = mass[...] * fade
    find_inverse(0)

    def send(step, sbuf, rbuf, sem, p):
        pltpu.make_async_remote_copy(
            src_ref=sbuf[step].at[p], dst_ref=rbuf[step].at[me], send_sem=sem.at[step, 0], recv_sem=sem.at[step, 1],
            device_id={"dom": lax.rem(me + p, doms)}, device_id_type=MESH,
        ).start()

    def whole(step, sbuf, rbuf, sem):
        return pltpu.make_async_remote_copy(
            src_ref=sbuf[step].at[pl.ds(1, doms - 1)], dst_ref=rbuf[step].at[pl.ds(1, doms - 1)],
            send_sem=sem.at[step, 0], recv_sem=sem.at[step, 1],
            device_id={"dom": lax.rem(me + 1, doms)}, device_id_type=MESH,
        )

    def send_carried(step, source):
        def load(p):
            return source(inverse[step, lax.rem(me + p, doms)])

        m, e = load(0)
        carried_recv[step][me, 0:2, :] = m
        carried_recv[step][me, 2:4, :] = e

        def one(p, _):
            m, e = load(p)
            carried_send[step][p, 0:2, :] = m
            carried_send[step][p, 2:4, :] = e
            send(step, carried_send, carried_recv, carried_sem, p)
            return 0

        lax.fori_loop(1, doms, one, 0, unroll=5 if doms == 16 else 1)

    send_carried(0, lambda j: (mass[j], decay[j]))

    tall_ids = lax.broadcasted_iota(jnp.int32, (LANES, width), 0).astype(BF16)
    cell_rows = lax.broadcasted_iota(jnp.int32, (rows, width), 0)
    home_rows = lax.broadcasted_iota(jnp.int32, (8, width), 0)

    def low_hits(cells):
        low = jnp.broadcast_to(lax.bitwise_and(cells, LANES - 1), (16, width)).astype(BF16)
        low = jnp.broadcast_to(low[None], (LANES // 16, 16, width)).reshape(LANES, width)
        return jnp.where(low == tall_ids, jnp.ones((), BF16), jnp.zeros((), BF16))

    def high_bits(cells):
        return lax.shift_right_logical(cells, 7)

    def deposits(step, blocks):
        weights, hits = [], []
        for j in blocks:
            cells = bed[step : step + 1, pl.ds(pl.multiple_of(j * width, width), width)]
            local = lax.div(tile[step, 0, j], doms)
            home = local * (BEDC // LANES) + high_bits(cells)
            amount = jnp.concatenate([dep[j, 0:1, :], dep[j, 1:2, :]], axis=1)
            weight = jnp.where(home == home_rows, amount, 0.0)
            high = weight.astype(BF16)
            low = (weight - high.astype(F32)).astype(BF16)
            weights.append(jnp.concatenate([high, low], axis=0))
            hits.append(low_hits(cells))
        return lax.dot_general(
            jnp.concatenate(weights, axis=1), jnp.concatenate(hits, axis=1),
            (((1,), (1,)), ((), ())), preferred_element_type=F32,
        )

    def all_deposits(step, total):
        def some(k, total):
            return total + deposits(step, [k * group + i for i in range(group)])

        return lax.fori_loop(0, nblocks // group, some, total)

    channel_ids = lax.broadcasted_iota(jnp.int32, (16, 2 * 4 * rows), 1) // rows % 4
    out_ids = lax.broadcasted_iota(jnp.int32, (16, 2 * 4 * rows), 0)
    mix = jnp.where(
        out_ids < 8,
        jnp.where(channel_ids == out_ids, 0.5 * time_step, 0.0),
        jnp.where(channel_ids == 3, time_step, 0.0),
    ).astype(BF16)

    def walk(step, blocks):
        picked = []
        for j in blocks:
            cells = cell[step : step + 1, pl.ds(pl.multiple_of(j * width, width), width)]
            row_hit = jnp.where(high_bits(cells) == cell_rows, 1.0, 0.0).astype(BF16)
            local = lax.div(tile[step, 0, j], doms)
            both = jnp.concatenate(
                [table[local, slab].reshape(4 * rows, LANES) for slab in (step, step + 1)], axis=0
            )
            found = jnp.dot(both, low_hits(cells), preferred_element_type=F32).astype(BF16)
            found = found.reshape(8, rows, width) * row_hit[None]
            picked.append(found.reshape(8 * rows, width))
        mixed = jnp.dot(mix, jnp.concatenate(picked, axis=1), preferred_element_type=F32)
        moves = []
        for i, j in enumerate(blocks):
            part = mixed[:, i * width : (i + 1) * width]
            draw = noise[step, :, pl.ds(pl.multiple_of(j * width, width), width)]
            moves.append(part[0:3] + jnp.sqrt(part[8:11]) * draw)
        return moves

    third = (lax.broadcasted_iota(jnp.int32, (3, width), 0) == 2)

    total = jnp.zeros((16, LANES), F32)

    for copy in staged[7:]:
        copy.wait()
    table_copy.wait_recv()

    def first(k, _):
        blocks = [k * group + i for i in range(group)]
        moves = walk(0, blocks)
        values = []
        for j, move in zip(blocks, moves):
            speed = jnp.concatenate([settle[j, 0:1, :], settle[j, 1:2, :]], axis=1)
            sink = jnp.where(third, steps * time_step * speed, 0.0)
            here = pos[:, pl.ds(pl.multiple_of(j * width, width), width)]
            values.append(here - sink + move)
        for j, value in zip(blocks, values):
            delta[j] = value
        return 0

    lax.fori_loop(0, nblocks // group, first, 0)

    def send_places(step, source):
        def one(p, _):
            pos_send[step][p] = source(inverse[step, lax.rem(me + p, doms)])
            send(step, pos_send, pos_recv, pos_sem, p)
            return 0

        lax.fori_loop(1, doms, one, 0, unroll=5 if doms == 16 else 1)
        pos_recv[step][me] = source(inverse[step, me])

    send_places(0, lambda j: delta[j])

    for step in range(1, steps):
        if step + 1 < steps:
            find_inverse(step)
        def some(k, total, step=step):
            blocks = [k * group + i for i in range(group)]
            moves = walk(step, blocks)
            total = total + deposits(step - 1, blocks)
            for j, move in zip(blocks, moves):
                delta[j] = move
            return total

        def forward(step=step):
            whole(step - 1, carried_send, carried_recv, carried_sem).wait_recv()

            def source(j):
                fade = carried_recv[step - 1][j, 2:4, :]
                return carried_recv[step - 1][j, 0:2, :] * fade, fade

            send_carried(step, source)

        if step + 1 < steps:
            forward()
        total = lax.fori_loop(0, nblocks // group, some, total)
        if step + 1 == steps:
            whole(step - 1, carried_send, carried_recv, carried_sem).wait_recv()
        masses = carried_recv[step - 1][:, 0:2, :]
        fade = carried_recv[step - 1][:, 2:4, :]
        left = masses * fade
        dep[...] = masses - left
        if step + 1 == steps:
            mass_out[...] = left
            total = all_deposits(step, total)
        if step + 1 == steps:
            for t in range(archs):
                q = BEDC // LANES
                bed_part[t] = (total[t * q : (t + 1) * q] + total[8 + t * q : 8 + (t + 1) * q]) * scale
            bed_copy = pltpu.make_async_remote_copy(
                src_ref=bed_part.at[twin], dst_ref=bed_recv, send_sem=bed_sem.at[0], recv_sem=bed_sem.at[1],
                device_id={"arch": twin}, device_id_type=MESH,
            )
            bed_copy.start()
        whole(step - 1, pos_send, pos_recv, pos_sem).wait_recv()
        if step + 1 < steps:
            send_places(step, lambda j, step=step: pos_recv[step - 1][j] + delta[j])

    last = steps - 2
    def finish(j, _):
        pos_out[:, pl.ds(pl.multiple_of(j * width, width), width)] = pos_recv[last][j] + delta[j]
        return 0

    lax.fori_loop(0, nblocks, finish, 0, unroll=16)
    bed_copy.wait_recv()
    bed_out[...] = bed_part[arch] + bed_recv[...]

    table_copy.wait_send()
    bed_copy.wait_send()
    for step in range(steps - 1):
        whole(step, carried_send, carried_recv, carried_sem).wait_send()
        whole(step, pos_send, pos_recv, pos_sem).wait_send()


def write_out(*refs):
    count = len(refs) // 2
    sem = refs[-1]
    copies = [pltpu.make_async_copy(refs[i], refs[count + i], sem.at[i]) for i in range(count)]
    for copy in copies:
        copy.start()
    for copy in copies:
        copy.wait()


def body(
    position, particle_mass, settling, walk_noise, velocity, diffusivity, block_tile, cell_index, bed_cell, route_code
):
    doms = lax.axis_size("dom")
    archs = lax.axis_size("arch")
    particles = position.shape[1]
    nblocks = block_tile.shape[2]
    width = particles // nblocks
    steps = cell_index.shape[0]
    slabs, _, _, cells = velocity.shape
    rows = cells // LANES
    half = width // LANES
    moves = steps - 1
    in_hbm = pl.BlockSpec(memory_space=pltpu.HBM)
    in_vmem = pl.BlockSpec(memory_space=pltpu.VMEM)
    vmem = pltpu.VMEM
    args = (
        position,
        particle_mass.reshape(nblocks, half, LANES),
        settling.reshape(nblocks, half, LANES),
        walk_noise,
        velocity.transpose(1, 2, 0, 3).reshape(3, slabs, cells),
        diffusivity.transpose(1, 0, 2).reshape(slabs, cells),
        block_tile,
        cell_index,
        bed_cell,
        route_code,
    )
    results = pl.pallas_call(
        functools.partial(
            kernel, doms, archs, nblocks, width, steps, slabs, rows, BEDC / particles
        ),
        out_shape=(
            pltpu.VMEM((3, particles), F32),
            pltpu.VMEM((nblocks, half, LANES), F32),
            pltpu.VMEM((BEDC // LANES, LANES), F32),
        ),
        in_specs=[in_hbm] * len(args),
        out_specs=(in_vmem, in_vmem, in_vmem),
        scratch_shapes=[
            vmem(args[0].shape, F32),
            vmem(args[1].shape, F32),
            vmem(args[2].shape, F32),
            vmem(args[3].shape, F32),
            vmem(args[4].shape, BF16),
            vmem(args[5].shape, BF16),
            pltpu.SMEM(args[6].shape, jnp.int32),
            vmem(args[7].shape, jnp.int32),
            vmem(args[8].shape, jnp.int32),
            pltpu.SMEM(args[9].shape, jnp.int32),
            vmem((4, slabs * rows, LANES), F32),
            vmem((archs, slabs, 4, rows, LANES), BF16),
            pltpu.SMEM((moves, nblocks), jnp.int32),
            vmem((nblocks, half, LANES), F32),
            vmem((nblocks, half, LANES), F32),
            vmem((nblocks, 3, width), F32),
            [vmem((nblocks, 2 * half, LANES), F32)] * moves,
            [vmem((nblocks, 2 * half, LANES), F32)] * moves,
            [vmem((nblocks, 3, width), F32)] * moves,
            [vmem((nblocks, 3, width), F32)] * moves,
            vmem((archs, BEDC // LANES, LANES), F32),
            vmem((BEDC // LANES, LANES), F32),
            pltpu.SemaphoreType.DMA((len(args),)),
            pltpu.SemaphoreType.DMA((2,)),
            pltpu.SemaphoreType.DMA((moves, 2)),
            pltpu.SemaphoreType.DMA((moves, 2)),
            pltpu.SemaphoreType.DMA((2,)),
        ],
        compiler_params=pltpu.CompilerParams(
            collective_id=0, has_side_effects=True, vmem_limit_bytes=60 * 1024 * 1024
        ),
    )(*args)
    places, masses, beds = pl.pallas_call(
        write_out,
        out_shape=tuple(jax.ShapeDtypeStruct(r.shape, F32) for r in results),
        in_specs=[in_vmem] * 3,
        out_specs=(in_hbm,) * 3,
        scratch_shapes=[pltpu.SemaphoreType.DMA((3,))],
    )(*(pltpu.with_memory_space_constraint(r, pltpu.VMEM) for r in results))
    return places, masses.reshape(particles), beds.reshape(1, BEDC)


def solution(mesh):
    return jax.shard_map(
        body,
        mesh=mesh,
        in_specs=(
            P(None, ("arch", "dom")),
            P(("arch", "dom")),
            P(("arch", "dom")),
            P(None, None, ("arch", "dom")),
            P(None, None, ("arch", "dom"), None),
            P(None, ("arch", "dom"), None),
            P(None, ("arch", "dom"), None),
            P(None, ("arch", "dom")),
            P(None, ("arch", "dom")),
            P(None, ("arch", "dom"), None),
        ),
        out_specs=(P(None, ("arch", "dom")), P(("arch", "dom")), P(("arch", "dom"), None)),
        check_vma=False,
    )
```

```python
import functools
import math

import jax
import jax.numpy as jnp
from jax import lax
from jax.experimental import pallas as pl
from jax.experimental.pallas import tpu as pltpu
from jax.sharding import PartitionSpec as P

MESH = pl.DeviceIdType.MESH
BF16 = jnp.bfloat16
F32 = jnp.float32

BEDC = 512
LANES = 128
time_step = 0.5


def kernel(
    doms, archs, nblocks, width, steps, slabs, rows, scale,
    pos_hbm, mass_hbm, settle_hbm, noise_hbm, vel_hbm, diff_hbm, tile_hbm, cell_hbm, bed_hbm, route_hbm,
    pos_out, mass_out, bed_out,
    pos, mass, settle, noise, vel, diff, far_vel, far_diff, tile, cell, bed, route,
    spread_rows, table, inverse, decay, dep, delta,
    carried_send, carried_recv, pos_send, pos_recv,
    bed_part, bed_recv,
    in_sem, table_sem, carried_sem, pos_sem, bed_sem,
):
    me = lax.axis_index("dom")
    arch = lax.axis_index("arch")
    twin = lax.rem(arch + 1, archs)
    group = math.gcd(nblocks, 16)

    staged = [
        pltpu.make_async_copy(src, dst, in_sem.at[i])
        for i, (src, dst) in enumerate(
            [
                (vel_hbm, vel), (diff_hbm, diff), (tile_hbm, tile), (route_hbm, route), (mass_hbm, mass),
                (settle_hbm, settle), (bed_hbm, bed), (cell_hbm, cell), (pos_hbm, pos), (noise_hbm, noise),
            ]
        )
    ]
    for copy in staged[:2]:
        copy.start()

    barrier = pltpu.get_barrier_semaphore()

    def greet(p, _):
        pl.semaphore_signal(barrier, inc=1, device_id={"dom": lax.rem(me + p, doms)}, device_id_type=MESH)
        return 0

    lax.fori_loop(1, doms, greet, 0)
    pl.semaphore_signal(barrier, inc=1, device_id={"arch": twin}, device_id_type=MESH)

    for copy in staged[2:]:
        copy.start()

    def find_inverse(step):
        def invert(c, _):
            def probe(j, found):
                return jnp.where(route[step, 0, j] == c, j, found)

            inverse[step, c] = lax.fori_loop(0, nblocks, probe, jnp.int32(0), unroll=True if nblocks <= 16 else 16)
            return 0

        lax.fori_loop(0, nblocks, invert, 0, unroll=4)

    def lay_out(owner, speeds, mixing):
        for ch in range(4):
            raw = (speeds[ch] if ch < 3 else mixing[...]).astype(F32)
            for r in range(rows):
                spread_rows[ch, pl.ds(r, slabs, stride=rows), :] = raw[:, r * LANES : (r + 1) * LANES]
        for slab in range(slabs):
            for ch in range(4):
                table[owner, slab, ch] = spread_rows[ch, slab * rows : (slab + 1) * rows, :].astype(BF16)

    pl.semaphore_wait(barrier, doms - 1 + archs - 1)

    tile_copies = [
        pltpu.make_async_remote_copy(
            src_ref=src, dst_ref=dst, send_sem=table_sem.at[i, 0], recv_sem=table_sem.at[i, 1],
            device_id={"arch": twin}, device_id_type=MESH,
        )
        for i, (src, dst) in enumerate([(vel_hbm, far_vel), (diff_hbm, far_diff)])
    ]
    for copy in tile_copies:
        copy.start()
    for copy in staged[:2]:
        copy.wait()
    lay_out(arch, vel, diff)

    for copy in staged[2:7]:
        copy.wait()
    fade = jnp.exp(-time_step * settle[...])
    decay[...] = fade
    dep[0][...] = mass[...] * (1.0 - fade)
    mass[...] = mass[...] * fade
    find_inverse(0)

    def send(step, sbuf, rbuf, sem, p):
        pltpu.make_async_remote_copy(
            src_ref=sbuf[step].at[p], dst_ref=rbuf[step].at[me], send_sem=sem.at[step, 0], recv_sem=sem.at[step, 1],
            device_id={"dom": lax.rem(me + p, doms)}, device_id_type=MESH,
        ).start()

    def whole(step, sbuf, rbuf, sem):
        return pltpu.make_async_remote_copy(
            src_ref=sbuf[step].at[pl.ds(1, doms - 1)], dst_ref=rbuf[step].at[pl.ds(1, doms - 1)],
            send_sem=sem.at[step, 0], recv_sem=sem.at[step, 1],
            device_id={"dom": lax.rem(me + 1, doms)}, device_id_type=MESH,
        )

    def send_carried(step, source):
        def load(p):
            return source(inverse[step, lax.rem(me + p, doms)])

        m, e = load(0)
        carried_recv[step][me, 0:2, :] = m
        carried_recv[step][me, 2:4, :] = e

        def one(p, _):
            m, e = load(p)
            carried_send[step][p, 0:2, :] = m
            carried_send[step][p, 2:4, :] = e
            send(step, carried_send, carried_recv, carried_sem, p)
            return 0

        lax.fori_loop(1, doms, one, 0, unroll=5 if doms == 16 else 1)

    send_carried(0, lambda j: (mass[j], decay[j]))

    tall_ids = lax.broadcasted_iota(jnp.int32, (LANES, width), 0).astype(BF16)
    cell_rows = lax.broadcasted_iota(jnp.int32, (rows, width), 0)
    home_rows = lax.broadcasted_iota(jnp.int32, (8, width), 0)

    def low_hits(cells):
        low = jnp.broadcast_to(lax.bitwise_and(cells, LANES - 1), (16, width)).astype(BF16)
        low = jnp.broadcast_to(low[None], (LANES // 16, 16, width)).reshape(LANES, width)
        return jnp.where(low == tall_ids, jnp.ones((), BF16), jnp.zeros((), BF16))

    def high_bits(cells):
        return lax.shift_right_logical(cells, 7)

    def deposits(step, blocks):
        weights, hits = [], []
        for j in blocks:
            cells = bed[step : step + 1, pl.ds(pl.multiple_of(j * width, width), width)]
            local = lax.div(tile[step, 0, j], doms)
            home = local * (BEDC // LANES) + high_bits(cells)
            amount = jnp.concatenate([dep[step][j, 0:1, :], dep[step][j, 1:2, :]], axis=1)
            weight = jnp.where(home == home_rows, amount, 0.0)
            high = weight.astype(BF16)
            low = (weight - high.astype(F32)).astype(BF16)
            weights.append(jnp.concatenate([high, low], axis=0))
            hits.append(low_hits(cells))
        return lax.dot_general(
            jnp.concatenate(weights, axis=1), jnp.concatenate(hits, axis=1),
            (((1,), (1,)), ((), ())), preferred_element_type=F32,
        )

    channel_ids = lax.broadcasted_iota(jnp.int32, (16, 2 * 4 * rows), 1) // rows % 4
    out_ids = lax.broadcasted_iota(jnp.int32, (16, 2 * 4 * rows), 0)
    mix = jnp.where(
        out_ids < 8,
        jnp.where(channel_ids == out_ids, 0.5 * time_step, 0.0),
        jnp.where(channel_ids == 3, time_step, 0.0),
    ).astype(BF16)

    def walk(step, blocks):
        picked = []
        for j in blocks:
            cells = cell[step : step + 1, pl.ds(pl.multiple_of(j * width, width), width)]
            row_hit = jnp.where(high_bits(cells) == cell_rows, 1.0, 0.0).astype(BF16)
            local = lax.div(tile[step, 0, j], doms)
            both = jnp.concatenate(
                [table[local, slab].reshape(4 * rows, LANES) for slab in (step, step + 1)], axis=0
            )
            found = jnp.dot(both, low_hits(cells), preferred_element_type=F32).astype(BF16)
            found = found.reshape(8, rows, width) * row_hit[None]
            picked.append(found.reshape(8 * rows, width))
        mixed = jnp.dot(mix, jnp.concatenate(picked, axis=1), preferred_element_type=F32)
        moves = []
        for i, j in enumerate(blocks):
            part = mixed[:, i * width : (i + 1) * width]
            draw = noise[step, :, pl.ds(pl.multiple_of(j * width, width), width)]
            moves.append(part[0:3] + jnp.sqrt(part[8:11]) * draw)
        return moves

    third = (lax.broadcasted_iota(jnp.int32, (3, width), 0) == 2)

    total = jnp.zeros((16, LANES), F32)

    for copy in staged[7:]:
        copy.wait()
    for copy in tile_copies:
        copy.wait_recv()
    lay_out(twin, far_vel, far_diff)

    def first(k, _):
        blocks = [k * group + i for i in range(group)]
        moves = walk(0, blocks)
        values = []
        for j, move in zip(blocks, moves):
            speed = jnp.concatenate([settle[j, 0:1, :], settle[j, 1:2, :]], axis=1)
            sink = jnp.where(third, steps * time_step * speed, 0.0)
            here = pos[:, pl.ds(pl.multiple_of(j * width, width), width)]
            values.append(here - sink + move)
        for j, value in zip(blocks, values):
            delta[j] = value
        return 0

    lax.fori_loop(0, nblocks // group, first, 0)

    def send_places(step, source):
        def one(p, _):
            pos_send[step][p] = source(inverse[step, lax.rem(me + p, doms)])
            send(step, pos_send, pos_recv, pos_sem, p)
            return 0

        lax.fori_loop(1, doms, one, 0, unroll=5 if doms == 16 else 1)
        pos_recv[step][me] = source(inverse[step, me])

    send_places(0, lambda j: delta[j])

    for step in range(1, steps):
        if step + 1 < steps:
            find_inverse(step)
        final = step + 1 == steps
        whole(step - 1, carried_send, carried_recv, carried_sem).wait_recv()
        masses = carried_recv[step - 1][:, 0:2, :]
        left = masses * carried_recv[step - 1][:, 2:4, :]
        dep[step][...] = masses - left
        if final:
            mass_out[...] = left
        else:
            def source(j, step=step):
                fade = carried_recv[step - 1][j, 2:4, :]
                return carried_recv[step - 1][j, 0:2, :] * fade, fade

            send_carried(step, source)

        def settle_down(k, total, step=step, final=final):
            blocks = [k * group + i for i in range(group)]
            total = total + deposits(step - 1, blocks)
            return total + deposits(step, blocks) if final else total

        def wander(k, total, step=step, final=final):
            blocks = [k * group + i for i in range(group)]
            moves = walk(step, blocks)
            if not final:
                total = settle_down(k, total, step, final)
            for j, move in zip(blocks, moves):
                delta[j] = move
            return total

        if final:
            total = lax.fori_loop(0, nblocks // group, settle_down, total)
            for t in range(archs):
                q = BEDC // LANES
                bed_part[t] = (total[t * q : (t + 1) * q] + total[8 + t * q : 8 + (t + 1) * q]) * scale
            bed_copy = pltpu.make_async_remote_copy(
                src_ref=bed_part.at[twin], dst_ref=bed_recv, send_sem=bed_sem.at[0], recv_sem=bed_sem.at[1],
                device_id={"arch": twin}, device_id_type=MESH,
            )
            bed_copy.start()
        total = lax.fori_loop(0, nblocks // group, wander, total)
        whole(step - 1, pos_send, pos_recv, pos_sem).wait_recv()
        if step + 1 < steps:
            send_places(step, lambda j, step=step: pos_recv[step - 1][j] + delta[j])

    last = steps - 2
    def finish(j, _):
        pos_out[:, pl.ds(pl.multiple_of(j * width, width), width)] = pos_recv[last][j] + delta[j]
        return 0

    lax.fori_loop(0, nblocks, finish, 0, unroll=16)
    bed_copy.wait_recv()
    bed_out[...] = bed_part[arch] + bed_recv[...]

    for copy in tile_copies:
        copy.wait_send()
    bed_copy.wait_send()
    for step in range(steps - 1):
        whole(step, carried_send, carried_recv, carried_sem).wait_send()
        whole(step, pos_send, pos_recv, pos_sem).wait_send()


def write_out(*refs):
    count = len(refs) // 2
    sem = refs[-1]
    copies = [pltpu.make_async_copy(refs[i], refs[count + i], sem.at[i]) for i in range(count)]
    for copy in copies:
        copy.start()
    for copy in copies:
        copy.wait()


def body(
    position, particle_mass, settling, walk_noise, velocity, diffusivity, block_tile, cell_index, bed_cell, route_code
):
    doms = lax.axis_size("dom")
    archs = lax.axis_size("arch")
    particles = position.shape[1]
    nblocks = block_tile.shape[2]
    width = particles // nblocks
    steps = cell_index.shape[0]
    slabs, _, _, cells = velocity.shape
    rows = cells // LANES
    half = width // LANES
    moves = steps - 1
    in_hbm = pl.BlockSpec(memory_space=pltpu.HBM)
    in_vmem = pl.BlockSpec(memory_space=pltpu.VMEM)
    vmem = pltpu.VMEM
    args = (
        position,
        particle_mass.reshape(nblocks, half, LANES),
        settling.reshape(nblocks, half, LANES),
        walk_noise,
        velocity.transpose(1, 2, 0, 3).reshape(3, slabs, cells),
        diffusivity.transpose(1, 0, 2).reshape(slabs, cells),
        block_tile,
        cell_index,
        bed_cell,
        route_code,
    )
    results = pl.pallas_call(
        functools.partial(
            kernel, doms, archs, nblocks, width, steps, slabs, rows, BEDC / particles
        ),
        out_shape=(
            pltpu.VMEM((3, particles), F32),
            pltpu.VMEM((nblocks, half, LANES), F32),
            pltpu.VMEM((BEDC // LANES, LANES), F32),
        ),
        in_specs=[in_hbm] * len(args),
        out_specs=(in_vmem, in_vmem, in_vmem),
        scratch_shapes=[
            vmem(args[0].shape, F32),
            vmem(args[1].shape, F32),
            vmem(args[2].shape, F32),
            vmem(args[3].shape, F32),
            vmem(args[4].shape, BF16),
            vmem(args[5].shape, BF16),
            vmem(args[4].shape, BF16),
            vmem(args[5].shape, BF16),
            pltpu.SMEM(args[6].shape, jnp.int32),
            vmem(args[7].shape, jnp.int32),
            vmem(args[8].shape, jnp.int32),
            pltpu.SMEM(args[9].shape, jnp.int32),
            vmem((4, slabs * rows, LANES), F32),
            vmem((archs, slabs, 4, rows, LANES), BF16),
            pltpu.SMEM((moves, nblocks), jnp.int32),
            vmem((nblocks, half, LANES), F32),
            [vmem((nblocks, half, LANES), F32)] * steps,
            vmem((nblocks, 3, width), F32),
            [vmem((nblocks, 2 * half, LANES), F32)] * moves,
            [vmem((nblocks, 2 * half, LANES), F32)] * moves,
            [vmem((nblocks, 3, width), F32)] * moves,
            [vmem((nblocks, 3, width), F32)] * moves,
            vmem((archs, BEDC // LANES, LANES), F32),
            vmem((BEDC // LANES, LANES), F32),
            pltpu.SemaphoreType.DMA((len(args),)),
            pltpu.SemaphoreType.DMA((2, 2)),
            pltpu.SemaphoreType.DMA((moves, 2)),
            pltpu.SemaphoreType.DMA((moves, 2)),
            pltpu.SemaphoreType.DMA((2,)),
        ],
        compiler_params=pltpu.CompilerParams(
            collective_id=0, has_side_effects=True, vmem_limit_bytes=60 * 1024 * 1024
        ),
    )(*args)
    places, masses, beds = pl.pallas_call(
        write_out,
        out_shape=tuple(jax.ShapeDtypeStruct(r.shape, F32) for r in results),
        in_specs=[in_vmem] * 3,
        out_specs=(in_hbm,) * 3,
        scratch_shapes=[pltpu.SemaphoreType.DMA((3,))],
    )(*(pltpu.with_memory_space_constraint(r, pltpu.VMEM) for r in results))
    return places, masses.reshape(particles), beds.reshape(1, BEDC)


def solution(mesh):
    return jax.shard_map(
        body,
        mesh=mesh,
        in_specs=(
            P(None, ("arch", "dom")),
            P(("arch", "dom")),
            P(("arch", "dom")),
            P(None, None, ("arch", "dom")),
            P(None, None, ("arch", "dom"), None),
            P(None, ("arch", "dom"), None),
            P(None, ("arch", "dom"), None),
            P(None, ("arch", "dom")),
            P(None, ("arch", "dom")),
            P(None, ("arch", "dom"), None),
        ),
        out_specs=(P(None, ("arch", "dom")), P(("arch", "dom")), P(("arch", "dom"), None)),
        check_vma=False,
    )
```

```python
import functools
import math

import jax
import jax.numpy as jnp
from jax import lax
from jax.experimental import pallas as pl
from jax.experimental.pallas import tpu as pltpu
from jax.sharding import PartitionSpec as P

MESH = pl.DeviceIdType.MESH
BF16 = jnp.bfloat16
F32 = jnp.float32

BEDC = 512
LANES = 128
time_step = 0.5


def kernel(
    doms, archs, nblocks, width, steps, slabs, rows, scale,
    pos_hbm, mass_hbm, settle_hbm, noise_hbm, vel_hbm, diff_hbm, tile_hbm, cell_hbm, bed_hbm, route_hbm,
    pos_out, mass_out, bed_out,
    pos, mass, settle, noise, vel, diff, tile, cell, bed, route,
    spread_rows, table, inverse, decay, dep, delta,
    carried_send, carried_recv, pos_send, pos_recv,
    bed_part, bed_recv,
    in_sem, table_sem, carried_sem, pos_sem, bed_sem,
):
    me = lax.axis_index("dom")
    arch = lax.axis_index("arch")
    twin = lax.rem(arch + 1, archs)
    group = math.gcd(nblocks, 16)

    staged = [
        pltpu.make_async_copy(src, dst, in_sem.at[i])
        for i, (src, dst) in enumerate(
            [
                (vel_hbm, vel), (diff_hbm, diff), (tile_hbm, tile), (route_hbm, route), (mass_hbm, mass),
                (settle_hbm, settle), (bed_hbm, bed), (cell_hbm, cell), (pos_hbm, pos), (noise_hbm, noise),
            ]
        )
    ]
    for copy in staged[:2]:
        copy.start()

    barrier = pltpu.get_barrier_semaphore()

    def greet(p, _):
        pl.semaphore_signal(barrier, inc=1, device_id={"dom": lax.rem(me + p, doms)}, device_id_type=MESH)
        return 0

    lax.fori_loop(1, doms, greet, 0)
    pl.semaphore_signal(barrier, inc=1, device_id={"arch": twin}, device_id_type=MESH)

    for copy in staged[2:]:
        copy.start()

    def find_inverse(step):
        def invert(c, _):
            def probe(j, found):
                return jnp.where(route[step, 0, j] == c, j, found)

            inverse[step, c] = lax.fori_loop(0, nblocks, probe, jnp.int32(0), unroll=True if nblocks <= 16 else 16)
            return 0

        lax.fori_loop(0, nblocks, invert, 0, unroll=4)

    for copy in staged[:2]:
        copy.wait()
    for ch in range(4):
        raw = (vel[ch] if ch < 3 else diff[...]).astype(F32)
        for r in range(rows):
            spread_rows[ch, pl.ds(r, slabs, stride=rows), :] = raw[:, r * LANES : (r + 1) * LANES]
    for slab in range(slabs):
        for ch in range(4):
            table[arch, slab, ch] = spread_rows[ch, slab * rows : (slab + 1) * rows, :].astype(BF16)

    pl.semaphore_wait(barrier, doms - 1 + archs - 1)

    table_copy = pltpu.make_async_remote_copy(
        src_ref=table.at[arch], dst_ref=table.at[arch], send_sem=table_sem.at[0], recv_sem=table_sem.at[1],
        device_id={"arch": twin}, device_id_type=MESH,
    )
    table_copy.start()

    for copy in staged[2:7]:
        copy.wait()
    fade = jnp.exp(-time_step * settle[...])
    decay[...] = fade
    dep[...] = mass[...] * (1.0 - fade)
    mass[...] = mass[...] * fade
    find_inverse(0)

    def send(step, sbuf, rbuf, sem, p):
        pltpu.make_async_remote_copy(
            src_ref=sbuf[step].at[p], dst_ref=rbuf[step].at[me], send_sem=sem.at[step, 0], recv_sem=sem.at[step, 1],
            device_id={"dom": lax.rem(me + p, doms)}, device_id_type=MESH,
        ).start()

    def whole(step, sbuf, rbuf, sem):
        return pltpu.make_async_remote_copy(
            src_ref=sbuf[step].at[pl.ds(1, doms - 1)], dst_ref=rbuf[step].at[pl.ds(1, doms - 1)],
            send_sem=sem.at[step, 0], recv_sem=sem.at[step, 1],
            device_id={"dom": lax.rem(me + 1, doms)}, device_id_type=MESH,
        )

    def send_carried(step, source):
        def load(p):
            return source(inverse[step, lax.rem(me + p, doms)])

        m, e = load(0)
        carried_recv[step][me, 0:2, :] = m
        carried_recv[step][me, 2:4, :] = e

        def one(p, _):
            m, e = load(p)
            carried_send[step][p, 0:2, :] = m
            carried_send[step][p, 2:4, :] = e
            send(step, carried_send, carried_recv, carried_sem, p)
            return 0

        lax.fori_loop(1, doms, one, 0, unroll=5 if doms == 16 else 1)

    send_carried(0, lambda j: (mass[j], decay[j]))

    tall_ids = lax.broadcasted_iota(jnp.int32, (LANES, width), 0).astype(BF16)
    cell_rows = lax.broadcasted_iota(jnp.int32, (rows, width), 0)
    home_rows = lax.broadcasted_iota(jnp.int32, (8, width), 0)

    def low_hits(cells):
        low = jnp.broadcast_to(lax.bitwise_and(cells, LANES - 1), (16, width)).astype(BF16)
        low = jnp.broadcast_to(low[None], (LANES // 16, 16, width)).reshape(LANES, width)
        return jnp.where(low == tall_ids, jnp.ones((), BF16), jnp.zeros((), BF16))

    def high_bits(cells):
        return lax.shift_right_logical(cells, 7)

    def deposits(step, blocks):
        weights, hits = [], []
        for j in blocks:
            cells = bed[step : step + 1, pl.ds(pl.multiple_of(j * width, width), width)]
            local = lax.div(tile[step, 0, j], doms)
            home = local * (BEDC // LANES) + high_bits(cells)
            amount = jnp.concatenate([dep[j, 0:1, :], dep[j, 1:2, :]], axis=1)
            weight = jnp.where(home == home_rows, amount, 0.0)
            high = weight.astype(BF16)
            low = (weight - high.astype(F32)).astype(BF16)
            weights.append(jnp.concatenate([high, low], axis=0))
            hits.append(low_hits(cells))
        return lax.dot_general(
            jnp.concatenate(hits, axis=1), jnp.concatenate(weights, axis=1),
            (((1,), (1,)), ((), ())), preferred_element_type=F32,
        )

    def all_deposits(step, total):
        def some(k, total):
            return total + deposits(step, [k * group + i for i in range(group)])

        return lax.fori_loop(0, nblocks // group, some, total)

    channel_ids = lax.broadcasted_iota(jnp.int32, (16, 2 * 4 * rows), 1) // rows % 4
    out_ids = lax.broadcasted_iota(jnp.int32, (16, 2 * 4 * rows), 0)
    mix = jnp.where(
        out_ids < 8,
        jnp.where(channel_ids == out_ids, 0.5 * time_step, 0.0),
        jnp.where(channel_ids == 3, time_step, 0.0),
    ).astype(BF16)

    def walk(step, blocks):
        picked = []
        for j in blocks:
            cells = cell[step : step + 1, pl.ds(pl.multiple_of(j * width, width), width)]
            row_hit = jnp.where(high_bits(cells) == cell_rows, 1.0, 0.0).astype(BF16)
            local = lax.div(tile[step, 0, j], doms)
            both = jnp.concatenate(
                [table[local, slab].reshape(4 * rows, LANES) for slab in (step, step + 1)], axis=0
            )
            found = jnp.dot(both, low_hits(cells), preferred_element_type=F32).astype(BF16)
            found = found.reshape(8, rows, width) * row_hit[None]
            picked.append(found.reshape(8 * rows, width))
        mixed = jnp.dot(mix, jnp.concatenate(picked, axis=1), preferred_element_type=F32)
        moves = []
        for i, j in enumerate(blocks):
            part = mixed[:, i * width : (i + 1) * width]
            draw = noise[step, :, pl.ds(pl.multiple_of(j * width, width), width)]
            moves.append(part[0:3] + jnp.sqrt(part[8:11]) * draw)
        return moves

    third = (lax.broadcasted_iota(jnp.int32, (3, width), 0) == 2)

    total = jnp.zeros((LANES, 16), F32)

    for copy in staged[7:]:
        copy.wait()
    table_copy.wait_recv()

    def first(k, _):
        blocks = [k * group + i for i in range(group)]
        moves = walk(0, blocks)
        values = []
        for j, move in zip(blocks, moves):
            speed = jnp.concatenate([settle[j, 0:1, :], settle[j, 1:2, :]], axis=1)
            sink = jnp.where(third, steps * time_step * speed, 0.0)
            here = pos[:, pl.ds(pl.multiple_of(j * width, width), width)]
            values.append(here - sink + move)
        for j, value in zip(blocks, values):
            delta[j] = value
        return 0

    lax.fori_loop(0, nblocks // group, first, 0)

    def send_places(step, source):
        def one(p, _):
            pos_send[step][p] = source(inverse[step, lax.rem(me + p, doms)])
            send(step, pos_send, pos_recv, pos_sem, p)
            return 0

        lax.fori_loop(1, doms, one, 0, unroll=5 if doms == 16 else 1)
        pos_recv[step][me] = source(inverse[step, me])

    send_places(0, lambda j: delta[j])

    for step in range(1, steps):
        if step + 1 < steps:
            find_inverse(step)
        def some(k, total, step=step):
            blocks = [k * group + i for i in range(group)]
            moves = walk(step, blocks)
            total = total + deposits(step - 1, blocks)
            for j, move in zip(blocks, moves):
                delta[j] = move
            return total

        def forward(step=step):
            whole(step - 1, carried_send, carried_recv, carried_sem).wait_recv()

            def source(j):
                fade = carried_recv[step - 1][j, 2:4, :]
                return carried_recv[step - 1][j, 0:2, :] * fade, fade

            send_carried(step, source)

        if step + 1 < steps:
            forward()
        total = lax.fori_loop(0, nblocks // group, some, total)
        if step + 1 == steps:
            whole(step - 1, carried_send, carried_recv, carried_sem).wait_recv()
        masses = carried_recv[step - 1][:, 0:2, :]
        fade = carried_recv[step - 1][:, 2:4, :]
        left = masses * fade
        dep[...] = masses - left
        if step + 1 == steps:
            mass_out[...] = left
            total = all_deposits(step, total)
        if step + 1 == steps:
            total = total.T
            for t in range(archs):
                q = BEDC // LANES
                bed_part[t] = (total[t * q : (t + 1) * q] + total[8 + t * q : 8 + (t + 1) * q]) * scale
            bed_copy = pltpu.make_async_remote_copy(
                src_ref=bed_part.at[twin], dst_ref=bed_recv, send_sem=bed_sem.at[0], recv_sem=bed_sem.at[1],
                device_id={"arch": twin}, device_id_type=MESH,
            )
            bed_copy.start()
        whole(step - 1, pos_send, pos_recv, pos_sem).wait_recv()
        if step + 1 < steps:
            send_places(step, lambda j, step=step: pos_recv[step - 1][j] + delta[j])

    last = steps - 2
    def finish(j, _):
        pos_out[:, pl.ds(pl.multiple_of(j * width, width), width)] = pos_recv[last][j] + delta[j]
        return 0

    lax.fori_loop(0, nblocks, finish, 0, unroll=16)
    bed_copy.wait_recv()
    bed_out[...] = bed_part[arch] + bed_recv[...]

    table_copy.wait_send()
    bed_copy.wait_send()
    for step in range(steps - 1):
        whole(step, carried_send, carried_recv, carried_sem).wait_send()
        whole(step, pos_send, pos_recv, pos_sem).wait_send()


def write_out(*refs):
    count = len(refs) // 2
    sem = refs[-1]
    copies = [pltpu.make_async_copy(refs[i], refs[count + i], sem.at[i]) for i in range(count)]
    for copy in copies:
        copy.start()
    for copy in copies:
        copy.wait()


def body(
    position, particle_mass, settling, walk_noise, velocity, diffusivity, block_tile, cell_index, bed_cell, route_code
):
    doms = lax.axis_size("dom")
    archs = lax.axis_size("arch")
    particles = position.shape[1]
    nblocks = block_tile.shape[2]
    width = particles // nblocks
    steps = cell_index.shape[0]
    slabs, _, _, cells = velocity.shape
    rows = cells // LANES
    half = width // LANES
    moves = steps - 1
    in_hbm = pl.BlockSpec(memory_space=pltpu.HBM)
    in_vmem = pl.BlockSpec(memory_space=pltpu.VMEM)
    vmem = pltpu.VMEM
    args = (
        position,
        particle_mass.reshape(nblocks, half, LANES),
        settling.reshape(nblocks, half, LANES),
        walk_noise,
        velocity.transpose(1, 2, 0, 3).reshape(3, slabs, cells),
        diffusivity.transpose(1, 0, 2).reshape(slabs, cells),
        block_tile,
        cell_index,
        bed_cell,
        route_code,
    )
    results = pl.pallas_call(
        functools.partial(
            kernel, doms, archs, nblocks, width, steps, slabs, rows, BEDC / particles
        ),
        out_shape=(
            pltpu.VMEM((3, particles), F32),
            pltpu.VMEM((nblocks, half, LANES), F32),
            pltpu.VMEM((BEDC // LANES, LANES), F32),
        ),
        in_specs=[in_hbm] * len(args),
        out_specs=(in_vmem, in_vmem, in_vmem),
        scratch_shapes=[
            vmem(args[0].shape, F32),
            vmem(args[1].shape, F32),
            vmem(args[2].shape, F32),
            vmem(args[3].shape, F32),
            vmem(args[4].shape, BF16),
            vmem(args[5].shape, BF16),
            pltpu.SMEM(args[6].shape, jnp.int32),
            vmem(args[7].shape, jnp.int32),
            vmem(args[8].shape, jnp.int32),
            pltpu.SMEM(args[9].shape, jnp.int32),
            vmem((4, slabs * rows, LANES), F32),
            vmem((archs, slabs, 4, rows, LANES), BF16),
            pltpu.SMEM((moves, nblocks), jnp.int32),
            vmem((nblocks, half, LANES), F32),
            vmem((nblocks, half, LANES), F32),
            vmem((nblocks, 3, width), F32),
            [vmem((nblocks, 2 * half, LANES), F32)] * moves,
            [vmem((nblocks, 2 * half, LANES), F32)] * moves,
            [vmem((nblocks, 3, width), F32)] * moves,
            [vmem((nblocks, 3, width), F32)] * moves,
            vmem((archs, BEDC // LANES, LANES), F32),
            vmem((BEDC // LANES, LANES), F32),
            pltpu.SemaphoreType.DMA((len(args),)),
            pltpu.SemaphoreType.DMA((2,)),
            pltpu.SemaphoreType.DMA((moves, 2)),
            pltpu.SemaphoreType.DMA((moves, 2)),
            pltpu.SemaphoreType.DMA((2,)),
        ],
        compiler_params=pltpu.CompilerParams(
            collective_id=0, has_side_effects=True, vmem_limit_bytes=60 * 1024 * 1024
        ),
    )(*args)
    places, masses, beds = pl.pallas_call(
        write_out,
        out_shape=tuple(jax.ShapeDtypeStruct(r.shape, F32) for r in results),
        in_specs=[in_vmem] * 3,
        out_specs=(in_hbm,) * 3,
        scratch_shapes=[pltpu.SemaphoreType.DMA((3,))],
    )(*(pltpu.with_memory_space_constraint(r, pltpu.VMEM) for r in results))
    return places, masses.reshape(particles), beds.reshape(1, BEDC)


def solution(mesh):
    return jax.shard_map(
        body,
        mesh=mesh,
        in_specs=(
            P(None, ("arch", "dom")),
            P(("arch", "dom")),
            P(("arch", "dom")),
            P(None, None, ("arch", "dom")),
            P(None, None, ("arch", "dom"), None),
            P(None, ("arch", "dom"), None),
            P(None, ("arch", "dom"), None),
            P(None, ("arch", "dom")),
            P(None, ("arch", "dom")),
            P(None, ("arch", "dom"), None),
        ),
        out_specs=(P(None, ("arch", "dom")), P(("arch", "dom")), P(("arch", "dom"), None)),
        check_vma=False,
    )
```

```python
import functools
import math

import jax
import jax.numpy as jnp
from jax import lax
from jax.experimental import pallas as pl
from jax.experimental.pallas import tpu as pltpu
from jax.sharding import PartitionSpec as P

MESH = pl.DeviceIdType.MESH
BF16 = jnp.bfloat16
F32 = jnp.float32

BEDC = 512
LANES = 128
time_step = 0.5


def kernel(
    doms, archs, nblocks, width, steps, slabs, rows, scale,
    pos_hbm, mass_hbm, settle_hbm, noise_hbm, vel_hbm, diff_hbm, tile_hbm, cell_hbm, bed_hbm, route_hbm,
    pos_out, mass_out, bed_out,
    pos, mass, settle, noise, vel, diff, tile, cell, bed, route,
    spread_rows, table, inverse, decay, dep, delta,
    carried_send, carried_recv, pos_send, pos_recv,
    bed_part, bed_recv,
    in_sem, table_sem, carried_sem, pos_sem, bed_sem,
):
    me = lax.axis_index("dom")
    arch = lax.axis_index("arch")
    twin = lax.rem(arch + 1, archs)
    group = math.gcd(nblocks, 16)

    staged = [
        pltpu.make_async_copy(src, dst, in_sem.at[i])
        for i, (src, dst) in enumerate(
            [
                (vel_hbm, vel), (diff_hbm, diff), (tile_hbm, tile), (route_hbm, route), (mass_hbm, mass),
                (settle_hbm, settle), (bed_hbm, bed), (cell_hbm, cell), (pos_hbm, pos), (noise_hbm, noise),
            ]
        )
    ]
    for copy in staged[:2]:
        copy.start()

    barrier = pltpu.get_barrier_semaphore()

    def greet(p, _):
        pl.semaphore_signal(barrier, inc=1, device_id={"dom": lax.rem(me + p, doms)}, device_id_type=MESH)
        return 0

    lax.fori_loop(1, doms, greet, 0)
    pl.semaphore_signal(barrier, inc=1, device_id={"arch": twin}, device_id_type=MESH)

    for copy in staged[2:]:
        copy.start()

    def find_inverse(step):
        def invert(c, _):
            def probe(j, found):
                return jnp.where(route[step, 0, j] == c, j, found)

            inverse[step, c] = lax.fori_loop(0, nblocks, probe, jnp.int32(0), unroll=True if nblocks <= 16 else 16)
            return 0

        lax.fori_loop(0, nblocks, invert, 0, unroll=4)

    for copy in staged[:2]:
        copy.wait()
    for ch in range(4):
        raw = (vel[ch] if ch < 3 else diff[...]).astype(F32)
        for r in range(rows):
            spread_rows[ch, pl.ds(r, slabs, stride=rows), :] = raw[:, r * LANES : (r + 1) * LANES]
    for slab in range(slabs):
        for ch in range(4):
            table[arch, slab, ch] = spread_rows[ch, slab * rows : (slab + 1) * rows, :].astype(BF16)

    pl.semaphore_wait(barrier, doms - 1 + archs - 1)

    table_copy = pltpu.make_async_remote_copy(
        src_ref=table.at[arch], dst_ref=table.at[arch], send_sem=table_sem.at[0], recv_sem=table_sem.at[1],
        device_id={"arch": twin}, device_id_type=MESH,
    )
    table_copy.start()

    for copy in staged[2:7]:
        copy.wait()
    fade = jnp.exp(-time_step * settle[...])
    decay[...] = fade
    dep[0][...] = mass[...] * (1.0 - fade)
    mass[...] = mass[...] * fade
    find_inverse(0)

    def send(step, sbuf, rbuf, sem, p):
        pltpu.make_async_remote_copy(
            src_ref=sbuf[step].at[p], dst_ref=rbuf[step].at[me], send_sem=sem.at[step, 0], recv_sem=sem.at[step, 1],
            device_id={"dom": lax.rem(me + p, doms)}, device_id_type=MESH,
        ).start()

    def whole(step, sbuf, rbuf, sem):
        return pltpu.make_async_remote_copy(
            src_ref=sbuf[step].at[pl.ds(1, doms - 1)], dst_ref=rbuf[step].at[pl.ds(1, doms - 1)],
            send_sem=sem.at[step, 0], recv_sem=sem.at[step, 1],
            device_id={"dom": lax.rem(me + 1, doms)}, device_id_type=MESH,
        )

    def send_carried(step, source):
        def load(p):
            return source(inverse[step, lax.rem(me + p, doms)])

        m, e = load(0)
        carried_recv[step][me, 0:2, :] = m
        carried_recv[step][me, 2:4, :] = e

        def one(p, _):
            m, e = load(p)
            carried_send[step][p, 0:2, :] = m
            carried_send[step][p, 2:4, :] = e
            send(step, carried_send, carried_recv, carried_sem, p)
            return 0

        lax.fori_loop(1, doms, one, 0, unroll=5 if doms == 16 else 1)

    send_carried(0, lambda j: (mass[j], decay[j]))

    tall_ids = lax.broadcasted_iota(jnp.int32, (LANES, width), 0).astype(BF16)
    cell_rows = lax.broadcasted_iota(jnp.int32, (rows, width), 0)
    home_rows = lax.broadcasted_iota(jnp.int32, (8, width), 0)

    def low_hits(cells):
        low = jnp.broadcast_to(lax.bitwise_and(cells, LANES - 1), (16, width)).astype(BF16)
        low = jnp.broadcast_to(low[None], (LANES // 16, 16, width)).reshape(LANES, width)
        return jnp.where(low == tall_ids, jnp.ones((), BF16), jnp.zeros((), BF16))

    def high_bits(cells):
        return lax.shift_right_logical(cells, 7)

    def deposits(step, blocks):
        weights, hits = [], []
        for j in blocks:
            cells = bed[step : step + 1, pl.ds(pl.multiple_of(j * width, width), width)]
            local = lax.div(tile[step, 0, j], doms)
            home = local * (BEDC // LANES) + high_bits(cells)
            amount = jnp.concatenate([dep[step][j, 0:1, :], dep[step][j, 1:2, :]], axis=1)
            weight = jnp.where(home == home_rows, amount, 0.0)
            high = weight.astype(BF16)
            low = (weight - high.astype(F32)).astype(BF16)
            weights.append(jnp.concatenate([high, low], axis=0))
            hits.append(low_hits(cells))
        return lax.dot_general(
            jnp.concatenate(hits, axis=1), jnp.concatenate(weights, axis=1),
            (((1,), (1,)), ((), ())), preferred_element_type=F32,
        )

    def all_deposits(those, total):
        def some(k, total):
            blocks = [k * group + i for i in range(group)]
            return total + sum(deposits(step, blocks) for step in those)

        return lax.fori_loop(0, nblocks // group, some, total)

    channel_ids = lax.broadcasted_iota(jnp.int32, (16, 2 * 4 * rows), 1) // rows % 4
    out_ids = lax.broadcasted_iota(jnp.int32, (16, 2 * 4 * rows), 0)
    mix = jnp.where(
        out_ids < 8,
        jnp.where(channel_ids == out_ids, 0.5 * time_step, 0.0),
        jnp.where(channel_ids == 3, time_step, 0.0),
    ).astype(BF16)

    def walk(step, blocks):
        picked = []
        for j in blocks:
            cells = cell[step : step + 1, pl.ds(pl.multiple_of(j * width, width), width)]
            row_hit = jnp.where(high_bits(cells) == cell_rows, 1.0, 0.0).astype(BF16)
            local = lax.div(tile[step, 0, j], doms)
            both = jnp.concatenate(
                [table[local, slab].reshape(4 * rows, LANES) for slab in (step, step + 1)], axis=0
            )
            found = jnp.dot(both, low_hits(cells), preferred_element_type=F32).astype(BF16)
            found = found.reshape(8, rows, width) * row_hit[None]
            picked.append(found.reshape(8 * rows, width))
        mixed = jnp.dot(mix, jnp.concatenate(picked, axis=1), preferred_element_type=F32)
        moves = []
        for i, j in enumerate(blocks):
            part = mixed[:, i * width : (i + 1) * width]
            draw = noise[step, :, pl.ds(pl.multiple_of(j * width, width), width)]
            moves.append(part[0:3] + jnp.sqrt(part[8:11]) * draw)
        return moves

    third = (lax.broadcasted_iota(jnp.int32, (3, width), 0) == 2)

    total = jnp.zeros((LANES, 16), F32)

    for copy in staged[7:]:
        copy.wait()
    table_copy.wait_recv()

    def first(k, _):
        blocks = [k * group + i for i in range(group)]
        moves = walk(0, blocks)
        values = []
        for j, move in zip(blocks, moves):
            speed = jnp.concatenate([settle[j, 0:1, :], settle[j, 1:2, :]], axis=1)
            sink = jnp.where(third, steps * time_step * speed, 0.0)
            here = pos[:, pl.ds(pl.multiple_of(j * width, width), width)]
            values.append(here - sink + move)
        for j, value in zip(blocks, values):
            delta[0][j] = value
        return 0

    lax.fori_loop(0, nblocks // group, first, 0)

    def send_places(step, source):
        def one(p, _):
            pos_send[step][p] = source(inverse[step, lax.rem(me + p, doms)])
            send(step, pos_send, pos_recv, pos_sem, p)
            return 0

        lax.fori_loop(1, doms, one, 0, unroll=5 if doms == 16 else 1)
        pos_recv[step][me] = source(inverse[step, me])

    send_places(0, lambda j: delta[0][j])

    for step in range(1, steps):
        if step + 1 < steps:
            find_inverse(step)
        final = step + 1 == steps
        whole(step - 1, carried_send, carried_recv, carried_sem).wait_recv()
        masses = carried_recv[step - 1][:, 0:2, :]
        left = masses * carried_recv[step - 1][:, 2:4, :]
        dep[step][...] = masses - left
        if final:
            mass_out[...] = left
        else:
            def source(j, step=step):
                fade = carried_recv[step - 1][j, 2:4, :]
                return carried_recv[step - 1][j, 0:2, :] * fade, fade

            send_carried(step, source)

        if step == 1:
            def wander(k, total):
                blocks = [k * group + i for i in range(group)]
                moves = [walk(later, blocks) for later in range(1, steps)]
                total = total + deposits(0, blocks)
                for later in range(1, steps):
                    for j, move in zip(blocks, moves[later - 1]):
                        delta[later][j] = move
                return total

            total = lax.fori_loop(0, nblocks // group, wander, total)
        if final:
            total = all_deposits(range(1, steps), total)
            total = total.T
            for t in range(archs):
                q = BEDC // LANES
                bed_part[t] = (total[t * q : (t + 1) * q] + total[8 + t * q : 8 + (t + 1) * q]) * scale
            bed_copy = pltpu.make_async_remote_copy(
                src_ref=bed_part.at[twin], dst_ref=bed_recv, send_sem=bed_sem.at[0], recv_sem=bed_sem.at[1],
                device_id={"arch": twin}, device_id_type=MESH,
            )
            bed_copy.start()
        whole(step - 1, pos_send, pos_recv, pos_sem).wait_recv()
        if step + 1 < steps:
            send_places(step, lambda j, step=step: pos_recv[step - 1][j] + delta[step][j])

    last = steps - 2
    def finish(j, _):
        pos_out[:, pl.ds(pl.multiple_of(j * width, width), width)] = pos_recv[last][j] + delta[last + 1][j]
        return 0

    lax.fori_loop(0, nblocks, finish, 0, unroll=16)
    bed_copy.wait_recv()
    bed_out[...] = bed_part[arch] + bed_recv[...]

    table_copy.wait_send()
    bed_copy.wait_send()
    for step in range(steps - 1):
        whole(step, carried_send, carried_recv, carried_sem).wait_send()
        whole(step, pos_send, pos_recv, pos_sem).wait_send()


def write_out(*refs):
    count = len(refs) // 2
    sem = refs[-1]
    copies = [pltpu.make_async_copy(refs[i], refs[count + i], sem.at[i]) for i in range(count)]
    for copy in copies:
        copy.start()
    for copy in copies:
        copy.wait()


def body(
    position, particle_mass, settling, walk_noise, velocity, diffusivity, block_tile, cell_index, bed_cell, route_code
):
    doms = lax.axis_size("dom")
    archs = lax.axis_size("arch")
    particles = position.shape[1]
    nblocks = block_tile.shape[2]
    width = particles // nblocks
    steps = cell_index.shape[0]
    slabs, _, _, cells = velocity.shape
    rows = cells // LANES
    half = width // LANES
    moves = steps - 1
    in_hbm = pl.BlockSpec(memory_space=pltpu.HBM)
    in_vmem = pl.BlockSpec(memory_space=pltpu.VMEM)
    vmem = pltpu.VMEM
    args = (
        position,
        particle_mass.reshape(nblocks, half, LANES),
        settling.reshape(nblocks, half, LANES),
        walk_noise,
        velocity.transpose(1, 2, 0, 3).reshape(3, slabs, cells),
        diffusivity.transpose(1, 0, 2).reshape(slabs, cells),
        block_tile,
        cell_index,
        bed_cell,
        route_code,
    )
    results = pl.pallas_call(
        functools.partial(
            kernel, doms, archs, nblocks, width, steps, slabs, rows, BEDC / particles
        ),
        out_shape=(
            pltpu.VMEM((3, particles), F32),
            pltpu.VMEM((nblocks, half, LANES), F32),
            pltpu.VMEM((BEDC // LANES, LANES), F32),
        ),
        in_specs=[in_hbm] * len(args),
        out_specs=(in_vmem, in_vmem, in_vmem),
        scratch_shapes=[
            vmem(args[0].shape, F32),
            vmem(args[1].shape, F32),
            vmem(args[2].shape, F32),
            vmem(args[3].shape, F32),
            vmem(args[4].shape, BF16),
            vmem(args[5].shape, BF16),
            pltpu.SMEM(args[6].shape, jnp.int32),
            vmem(args[7].shape, jnp.int32),
            vmem(args[8].shape, jnp.int32),
            pltpu.SMEM(args[9].shape, jnp.int32),
            vmem((4, slabs * rows, LANES), F32),
            vmem((archs, slabs, 4, rows, LANES), BF16),
            pltpu.SMEM((moves, nblocks), jnp.int32),
            vmem((nblocks, half, LANES), F32),
            [vmem((nblocks, half, LANES), F32)] * steps,
            [vmem((nblocks, 3, width), F32)] * steps,
            [vmem((nblocks, 2 * half, LANES), F32)] * moves,
            [vmem((nblocks, 2 * half, LANES), F32)] * moves,
            [vmem((nblocks, 3, width), F32)] * moves,
            [vmem((nblocks, 3, width), F32)] * moves,
            vmem((archs, BEDC // LANES, LANES), F32),
            vmem((BEDC // LANES, LANES), F32),
            pltpu.SemaphoreType.DMA((len(args),)),
            pltpu.SemaphoreType.DMA((2,)),
            pltpu.SemaphoreType.DMA((moves, 2)),
            pltpu.SemaphoreType.DMA((moves, 2)),
            pltpu.SemaphoreType.DMA((2,)),
        ],
        compiler_params=pltpu.CompilerParams(
            collective_id=0, has_side_effects=True, vmem_limit_bytes=60 * 1024 * 1024
        ),
    )(*args)
    places, masses, beds = pl.pallas_call(
        write_out,
        out_shape=tuple(jax.ShapeDtypeStruct(r.shape, F32) for r in results),
        in_specs=[in_vmem] * 3,
        out_specs=(in_hbm,) * 3,
        scratch_shapes=[pltpu.SemaphoreType.DMA((3,))],
    )(*(pltpu.with_memory_space_constraint(r, pltpu.VMEM) for r in results))
    return places, masses.reshape(particles), beds.reshape(1, BEDC)


def solution(mesh):
    return jax.shard_map(
        body,
        mesh=mesh,
        in_specs=(
            P(None, ("arch", "dom")),
            P(("arch", "dom")),
            P(("arch", "dom")),
            P(None, None, ("arch", "dom")),
            P(None, None, ("arch", "dom"), None),
            P(None, ("arch", "dom"), None),
            P(None, ("arch", "dom"), None),
            P(None, ("arch", "dom")),
            P(None, ("arch", "dom")),
            P(None, ("arch", "dom"), None),
        ),
        out_specs=(P(None, ("arch", "dom")), P(("arch", "dom")), P(("arch", "dom"), None)),
        check_vma=False,
    )
```

```python
import functools
import math

import jax
import jax.numpy as jnp
from jax import lax
from jax.experimental import pallas as pl
from jax.experimental.pallas import tpu as pltpu
from jax.sharding import PartitionSpec as P

MESH = pl.DeviceIdType.MESH
BF16 = jnp.bfloat16
F32 = jnp.float32

BEDC = 512
LANES = 128
time_step = 0.5


def kernel(
    doms, archs, nblocks, width, steps, slabs, rows, scale,
    pos_hbm, mass_hbm, settle_hbm, noise_hbm, vel_hbm, diff_hbm, tile_hbm, cell_hbm, bed_hbm, route_hbm,
    pos_out, mass_out, bed_out,
    pos, mass, settle, noise, vel, diff, tile, cell, bed, route,
    spread_rows, table, inverse, decay, dep, delta,
    carried_send, carried_recv, pos_send, pos_recv,
    bed_part, bed_recv,
    in_sem, table_sem, carried_sem, pos_sem, bed_sem,
):
    me = lax.axis_index("dom")
    arch = lax.axis_index("arch")
    twin = lax.rem(arch + 1, archs)
    group = math.gcd(nblocks, 16)

    staged = [
        pltpu.make_async_copy(src, dst, in_sem.at[i])
        for i, (src, dst) in enumerate(
            [
                (vel_hbm, vel), (diff_hbm, diff), (tile_hbm, tile), (route_hbm, route), (mass_hbm, mass),
                (settle_hbm, settle), (bed_hbm, bed), (cell_hbm, cell), (pos_hbm, pos), (noise_hbm, noise),
            ]
        )
    ]
    for copy in staged[:2]:
        copy.start()

    barrier = pltpu.get_barrier_semaphore()

    def greet(p, _):
        pl.semaphore_signal(barrier, inc=1, device_id={"dom": lax.rem(me + p, doms)}, device_id_type=MESH)
        return 0

    lax.fori_loop(1, doms, greet, 0)
    pl.semaphore_signal(barrier, inc=1, device_id={"arch": twin}, device_id_type=MESH)

    for copy in staged[2:]:
        copy.start()

    def find_inverse(step):
        def invert(c, _):
            def probe(j, found):
                return jnp.where(route[step, 0, j] == c, j, found)

            inverse[step, c] = lax.fori_loop(0, nblocks, probe, jnp.int32(0), unroll=True if nblocks <= 16 else 16)
            return 0

        lax.fori_loop(0, nblocks, invert, 0, unroll=4)

    for copy in staged[:2]:
        copy.wait()
    for ch in range(4):
        raw = (vel[ch] if ch < 3 else diff[...]).astype(F32)
        for r in range(rows):
            spread_rows[ch, pl.ds(r, slabs, stride=rows), :] = raw[:, r * LANES : (r + 1) * LANES]
    for slab in range(slabs):
        for ch in range(4):
            table[arch, slab, ch] = spread_rows[ch, slab * rows : (slab + 1) * rows, :].astype(BF16)

    pl.semaphore_wait(barrier, doms - 1 + archs - 1)

    table_copy = pltpu.make_async_remote_copy(
        src_ref=table.at[arch], dst_ref=table.at[arch], send_sem=table_sem.at[0], recv_sem=table_sem.at[1],
        device_id={"arch": twin}, device_id_type=MESH,
    )
    table_copy.start()

    for copy in staged[2:7]:
        copy.wait()
    fade = jnp.exp(-time_step * settle[...])
    decay[...] = fade
    dep[...] = mass[...] * (1.0 - fade)
    mass[...] = mass[...] * fade
    find_inverse(0)

    def send(step, sbuf, rbuf, sem, p):
        pltpu.make_async_remote_copy(
            src_ref=sbuf[step].at[p], dst_ref=rbuf[step].at[me], send_sem=sem.at[step, 0], recv_sem=sem.at[step, 1],
            device_id={"dom": lax.rem(me + p, doms)}, device_id_type=MESH,
        ).start()

    def whole(step, sbuf, rbuf, sem):
        return pltpu.make_async_remote_copy(
            src_ref=sbuf[step].at[pl.ds(1, doms - 1)], dst_ref=rbuf[step].at[pl.ds(1, doms - 1)],
            send_sem=sem.at[step, 0], recv_sem=sem.at[step, 1],
            device_id={"dom": lax.rem(me + 1, doms)}, device_id_type=MESH,
        )

    def send_carried(step, source):
        def load(p):
            return source(inverse[step, lax.rem(me + p, doms)])

        m, e = load(0)
        carried_recv[step][me, 0:2, :] = m
        carried_recv[step][me, 2:4, :] = e

        def one(p, _):
            m, e = load(p)
            carried_send[step][p, 0:2, :] = m
            carried_send[step][p, 2:4, :] = e
            send(step, carried_send, carried_recv, carried_sem, p)
            return 0

        lax.fori_loop(1, doms, one, 0, unroll=5 if doms == 16 else 1)

    send_carried(0, lambda j: (mass[j], decay[j]))

    tall_ids = lax.broadcasted_iota(jnp.int32, (LANES, width), 0).astype(BF16)
    cell_rows = lax.broadcasted_iota(jnp.int32, (rows, width), 0)
    home_rows = lax.broadcasted_iota(jnp.int32, (8, width), 0)

    def low_hits(cells):
        low = jnp.broadcast_to(lax.bitwise_and(cells, LANES - 1), (16, width)).astype(BF16)
        low = jnp.broadcast_to(low[None], (LANES // 16, 16, width)).reshape(LANES, width)
        return jnp.where(low == tall_ids, jnp.ones((), BF16), jnp.zeros((), BF16))

    def high_bits(cells):
        return lax.shift_right_logical(cells, 7)

    def deposits(step, blocks):
        weights, hits = [], []
        for j in blocks:
            cells = bed[step : step + 1, pl.ds(pl.multiple_of(j * width, width), width)]
            local = lax.div(tile[step, 0, j], doms)
            home = local * (BEDC // LANES) + high_bits(cells)
            amount = jnp.concatenate([dep[j, 0:1, :], dep[j, 1:2, :]], axis=1)
            weight = jnp.where(home == home_rows, amount, 0.0)
            high = weight.astype(BF16)
            low = (weight - high.astype(F32)).astype(BF16)
            weights.append(jnp.concatenate([high, low], axis=0))
            hits.append(low_hits(cells))
        return lax.dot_general(
            jnp.concatenate(hits, axis=1), jnp.concatenate(weights, axis=1),
            (((1,), (1,)), ((), ())), preferred_element_type=F32,
        )

    def all_deposits(step, total):
        def some(k, total):
            return total + deposits(step, [k * group + i for i in range(group)])

        return lax.fori_loop(0, nblocks // group, some, total)

    place_rows = lax.broadcasted_iota(jnp.int32, (3, width), 0)

    def walk(step, blocks):
        moves = []
        for j in blocks:
            cells = cell[step : step + 1, pl.ds(pl.multiple_of(j * width, width), width)]
            row_hit = high_bits(cells) == cell_rows
            local = lax.div(tile[step, 0, j], doms)
            both = jnp.concatenate(
                [table[local, slab].reshape(4 * rows, LANES) for slab in (step, step + 1)], axis=0
            )
            found = jnp.dot(both, low_hits(cells), preferred_element_type=F32)
            found = found.reshape(2, 4, rows, width)
            sums = [
                jnp.sum(jnp.where(row_hit, found[0, ch] + found[1, ch], 0.0), axis=0, keepdims=True)
                for ch in range(4)
            ]
            drift = jnp.where(place_rows == 0, sums[0], jnp.where(place_rows == 1, sums[1], sums[2]))
            draw = noise[step, :, pl.ds(pl.multiple_of(j * width, width), width)]
            moves.append(0.5 * time_step * drift + jnp.sqrt(time_step * sums[3]) * draw)
        return moves

    third = (lax.broadcasted_iota(jnp.int32, (3, width), 0) == 2)

    total = jnp.zeros((LANES, 16), F32)

    for copy in staged[7:]:
        copy.wait()
    table_copy.wait_recv()

    def first(k, _):
        blocks = [k * group + i for i in range(group)]
        moves = walk(0, blocks)
        values = []
        for j, move in zip(blocks, moves):
            speed = jnp.concatenate([settle[j, 0:1, :], settle[j, 1:2, :]], axis=1)
            sink = jnp.where(third, steps * time_step * speed, 0.0)
            here = pos[:, pl.ds(pl.multiple_of(j * width, width), width)]
            values.append(here - sink + move)
        for j, value in zip(blocks, values):
            delta[j] = value
        return 0

    lax.fori_loop(0, nblocks // group, first, 0)

    def send_places(step, source):
        def one(p, _):
            pos_send[step][p] = source(inverse[step, lax.rem(me + p, doms)])
            send(step, pos_send, pos_recv, pos_sem, p)
            return 0

        lax.fori_loop(1, doms, one, 0, unroll=5 if doms == 16 else 1)
        pos_recv[step][me] = source(inverse[step, me])

    send_places(0, lambda j: delta[j])

    for step in range(1, steps):
        if step + 1 < steps:
            find_inverse(step)
        def some(k, total, step=step):
            blocks = [k * group + i for i in range(group)]
            moves = walk(step, blocks)
            total = total + deposits(step - 1, blocks)
            for j, move in zip(blocks, moves):
                delta[j] = move
            return total

        def forward(step=step):
            whole(step - 1, carried_send, carried_recv, carried_sem).wait_recv()

            def source(j):
                fade = carried_recv[step - 1][j, 2:4, :]
                return carried_recv[step - 1][j, 0:2, :] * fade, fade

            send_carried(step, source)

        if step + 1 < steps:
            forward()
        total = lax.fori_loop(0, nblocks // group, some, total)
        if step + 1 == steps:
            whole(step - 1, carried_send, carried_recv, carried_sem).wait_recv()
        masses = carried_recv[step - 1][:, 0:2, :]
        fade = carried_recv[step - 1][:, 2:4, :]
        left = masses * fade
        dep[...] = masses - left
        if step + 1 == steps:
            mass_out[...] = left
            total = all_deposits(step, total)
        if step + 1 == steps:
            total = total.T
            for t in range(archs):
                q = BEDC // LANES
                bed_part[t] = (total[t * q : (t + 1) * q] + total[8 + t * q : 8 + (t + 1) * q]) * scale
            bed_copy = pltpu.make_async_remote_copy(
                src_ref=bed_part.at[twin], dst_ref=bed_recv, send_sem=bed_sem.at[0], recv_sem=bed_sem.at[1],
                device_id={"arch": twin}, device_id_type=MESH,
            )
            bed_copy.start()
        whole(step - 1, pos_send, pos_recv, pos_sem).wait_recv()
        if step + 1 < steps:
            send_places(step, lambda j, step=step: pos_recv[step - 1][j] + delta[j])

    last = steps - 2
    def finish(j, _):
        pos_out[:, pl.ds(pl.multiple_of(j * width, width), width)] = pos_recv[last][j] + delta[j]
        return 0

    lax.fori_loop(0, nblocks, finish, 0, unroll=16)
    bed_copy.wait_recv()
    bed_out[...] = bed_part[arch] + bed_recv[...]

    table_copy.wait_send()
    bed_copy.wait_send()
    for step in range(steps - 1):
        whole(step, carried_send, carried_recv, carried_sem).wait_send()
        whole(step, pos_send, pos_recv, pos_sem).wait_send()


def write_out(*refs):
    count = len(refs) // 2
    sem = refs[-1]
    copies = [pltpu.make_async_copy(refs[i], refs[count + i], sem.at[i]) for i in range(count)]
    for copy in copies:
        copy.start()
    for copy in copies:
        copy.wait()


def body(
    position, particle_mass, settling, walk_noise, velocity, diffusivity, block_tile, cell_index, bed_cell, route_code
):
    doms = lax.axis_size("dom")
    archs = lax.axis_size("arch")
    particles = position.shape[1]
    nblocks = block_tile.shape[2]
    width = particles // nblocks
    steps = cell_index.shape[0]
    slabs, _, _, cells = velocity.shape
    rows = cells // LANES
    half = width // LANES
    moves = steps - 1
    in_hbm = pl.BlockSpec(memory_space=pltpu.HBM)
    in_vmem = pl.BlockSpec(memory_space=pltpu.VMEM)
    vmem = pltpu.VMEM
    args = (
        position,
        particle_mass.reshape(nblocks, half, LANES),
        settling.reshape(nblocks, half, LANES),
        walk_noise,
        velocity.transpose(1, 2, 0, 3).reshape(3, slabs, cells),
        diffusivity.transpose(1, 0, 2).reshape(slabs, cells),
        block_tile,
        cell_index,
        bed_cell,
        route_code,
    )
    results = pl.pallas_call(
        functools.partial(
            kernel, doms, archs, nblocks, width, steps, slabs, rows, BEDC / particles
        ),
        out_shape=(
            pltpu.VMEM((3, particles), F32),
            pltpu.VMEM((nblocks, half, LANES), F32),
            pltpu.VMEM((BEDC // LANES, LANES), F32),
        ),
        in_specs=[in_hbm] * len(args),
        out_specs=(in_vmem, in_vmem, in_vmem),
        scratch_shapes=[
            vmem(args[0].shape, F32),
            vmem(args[1].shape, F32),
            vmem(args[2].shape, F32),
            vmem(args[3].shape, F32),
            vmem(args[4].shape, BF16),
            vmem(args[5].shape, BF16),
            pltpu.SMEM(args[6].shape, jnp.int32),
            vmem(args[7].shape, jnp.int32),
            vmem(args[8].shape, jnp.int32),
            pltpu.SMEM(args[9].shape, jnp.int32),
            vmem((4, slabs * rows, LANES), F32),
            vmem((archs, slabs, 4, rows, LANES), BF16),
            pltpu.SMEM((moves, nblocks), jnp.int32),
            vmem((nblocks, half, LANES), F32),
            vmem((nblocks, half, LANES), F32),
            vmem((nblocks, 3, width), F32),
            [vmem((nblocks, 2 * half, LANES), F32)] * moves,
            [vmem((nblocks, 2 * half, LANES), F32)] * moves,
            [vmem((nblocks, 3, width), F32)] * moves,
            [vmem((nblocks, 3, width), F32)] * moves,
            vmem((archs, BEDC // LANES, LANES), F32),
            vmem((BEDC // LANES, LANES), F32),
            pltpu.SemaphoreType.DMA((len(args),)),
            pltpu.SemaphoreType.DMA((2,)),
            pltpu.SemaphoreType.DMA((moves, 2)),
            pltpu.SemaphoreType.DMA((moves, 2)),
            pltpu.SemaphoreType.DMA((2,)),
        ],
        compiler_params=pltpu.CompilerParams(
            collective_id=0, has_side_effects=True, vmem_limit_bytes=60 * 1024 * 1024
        ),
    )(*args)
    places, masses, beds = pl.pallas_call(
        write_out,
        out_shape=tuple(jax.ShapeDtypeStruct(r.shape, F32) for r in results),
        in_specs=[in_vmem] * 3,
        out_specs=(in_hbm,) * 3,
        scratch_shapes=[pltpu.SemaphoreType.DMA((3,))],
    )(*(pltpu.with_memory_space_constraint(r, pltpu.VMEM) for r in results))
    return places, masses.reshape(particles), beds.reshape(1, BEDC)


def solution(mesh):
    return jax.shard_map(
        body,
        mesh=mesh,
        in_specs=(
            P(None, ("arch", "dom")),
            P(("arch", "dom")),
            P(("arch", "dom")),
            P(None, None, ("arch", "dom")),
            P(None, None, ("arch", "dom"), None),
            P(None, ("arch", "dom"), None),
            P(None, ("arch", "dom"), None),
            P(None, ("arch", "dom")),
            P(None, ("arch", "dom")),
            P(None, ("arch", "dom"), None),
        ),
        out_specs=(P(None, ("arch", "dom")), P(("arch", "dom")), P(("arch", "dom"), None)),
        check_vma=False,
    )
```

```python
import functools
import math

import jax
import jax.numpy as jnp
from jax import lax
from jax.experimental import pallas as pl
from jax.experimental.pallas import tpu as pltpu
from jax.sharding import PartitionSpec as P

MESH = pl.DeviceIdType.MESH
BF16 = jnp.bfloat16
F32 = jnp.float32

BEDC = 512
LANES = 128
time_step = 0.5


def kernel(
    doms, archs, nblocks, width, steps, slabs, rows, scale,
    pos_hbm, mass_hbm, settle_hbm, noise_hbm, vel_hbm, diff_hbm, tile_hbm, cell_hbm, bed_hbm, route_hbm,
    pos_out, mass_out, bed_out,
    pos, mass, settle, noise, vel, diff, tile, cell, bed, route,
    spread_rows, table, inverse, decay, dep, delta,
    carried_send, carried_recv, pos_send, pos_recv,
    bed_part, bed_recv,
    in_sem, table_sem, carried_sem, pos_sem, bed_sem,
):
    me = lax.axis_index("dom")
    arch = lax.axis_index("arch")
    twin = lax.rem(arch + 1, archs)
    group = math.gcd(nblocks, 16)

    staged = [
        pltpu.make_async_copy(src, dst, in_sem.at[i])
        for i, (src, dst) in enumerate(
            [
                (vel_hbm, vel), (diff_hbm, diff), (tile_hbm, tile), (route_hbm, route), (mass_hbm, mass),
                (settle_hbm, settle), (bed_hbm, bed), (cell_hbm, cell), (pos_hbm, pos), (noise_hbm, noise),
            ]
        )
    ]
    for copy in staged[:2]:
        copy.start()

    barrier = pltpu.get_barrier_semaphore()

    def greet(p, _):
        pl.semaphore_signal(barrier, inc=1, device_id={"dom": lax.rem(me + p, doms)}, device_id_type=MESH)
        return 0

    lax.fori_loop(1, doms, greet, 0)
    pl.semaphore_signal(barrier, inc=1, device_id={"arch": twin}, device_id_type=MESH)

    for copy in staged[2:]:
        copy.start()

    def find_inverse(step):
        def invert(c, _):
            def probe(j, found):
                return jnp.where(route[step, 0, j] == c, j, found)

            inverse[step, c] = lax.fori_loop(0, nblocks, probe, jnp.int32(0), unroll=True if nblocks <= 16 else 16)
            return 0

        lax.fori_loop(0, nblocks, invert, 0, unroll=4)

    for copy in staged[:2]:
        copy.wait()
    for ch in range(4):
        raw = (vel[ch] if ch < 3 else diff[...]).astype(F32)
        for r in range(rows):
            spread_rows[ch, pl.ds(r, slabs, stride=rows), :] = raw[:, r * LANES : (r + 1) * LANES]
    for slab in range(slabs):
        for ch in range(4):
            table[arch, slab, ch] = spread_rows[ch, slab * rows : (slab + 1) * rows, :].astype(BF16)

    pl.semaphore_wait(barrier, doms - 1 + archs - 1)

    table_copy = pltpu.make_async_remote_copy(
        src_ref=table.at[arch], dst_ref=table.at[arch], send_sem=table_sem.at[0], recv_sem=table_sem.at[1],
        device_id={"arch": twin}, device_id_type=MESH,
    )
    table_copy.start()

    for copy in staged[2:7]:
        copy.wait()
    fade = jnp.exp(-time_step * settle[...])
    decay[...] = fade
    dep[0][...] = mass[...] * (1.0 - fade)
    mass[...] = mass[...] * fade
    find_inverse(0)

    def send(step, sbuf, rbuf, sem, p):
        pltpu.make_async_remote_copy(
            src_ref=sbuf[step].at[p], dst_ref=rbuf[step].at[me], send_sem=sem.at[step, 0], recv_sem=sem.at[step, 1],
            device_id={"dom": lax.rem(me + p, doms)}, device_id_type=MESH,
        ).start()

    def whole(step, sbuf, rbuf, sem):
        return pltpu.make_async_remote_copy(
            src_ref=sbuf[step].at[pl.ds(1, doms - 1)], dst_ref=rbuf[step].at[pl.ds(1, doms - 1)],
            send_sem=sem.at[step, 0], recv_sem=sem.at[step, 1],
            device_id={"dom": lax.rem(me + 1, doms)}, device_id_type=MESH,
        )

    def send_carried(step, source):
        def load(p):
            return source(inverse[step, lax.rem(me + p, doms)])

        m, e = load(0)
        carried_recv[step][me, 0:2, :] = m
        carried_recv[step][me, 2:4, :] = e

        def one(p, _):
            m, e = load(p)
            carried_send[step][p, 0:2, :] = m
            carried_send[step][p, 2:4, :] = e
            send(step, carried_send, carried_recv, carried_sem, p)
            return 0

        lax.fori_loop(1, doms, one, 0, unroll=5 if doms == 16 else 1)

    send_carried(0, lambda j: (mass[j], decay[j]))

    tall_ids = lax.broadcasted_iota(jnp.int32, (LANES, width), 0).astype(BF16)
    cell_rows = lax.broadcasted_iota(jnp.int32, (rows, width), 0)
    home_rows = lax.broadcasted_iota(jnp.int32, (8, width), 0)

    def low_hits(cells):
        low = jnp.broadcast_to(lax.bitwise_and(cells, LANES - 1), (16, width)).astype(BF16)
        low = jnp.broadcast_to(low[None], (LANES // 16, 16, width)).reshape(LANES, width)
        return jnp.where(low == tall_ids, jnp.ones((), BF16), jnp.zeros((), BF16))

    def high_bits(cells):
        return lax.shift_right_logical(cells, 7)

    def deposits(step, blocks):
        weights, hits = [], []
        for j in blocks:
            cells = bed[step : step + 1, pl.ds(pl.multiple_of(j * width, width), width)]
            local = lax.div(tile[step, 0, j], doms)
            home = local * (BEDC // LANES) + high_bits(cells)
            amount = jnp.concatenate([dep[step][j, 0:1, :], dep[step][j, 1:2, :]], axis=1)
            weight = jnp.where(home == home_rows, amount, 0.0)
            high = weight.astype(BF16)
            low = (weight - high.astype(F32)).astype(BF16)
            weights.append(jnp.concatenate([high, low], axis=0))
            hits.append(low_hits(cells))
        return lax.dot_general(
            jnp.concatenate(hits, axis=1), jnp.concatenate(weights, axis=1),
            (((1,), (1,)), ((), ())), preferred_element_type=F32,
        )

    def all_deposits(step, total):
        def some(k, total):
            return total + deposits(step, [k * group + i for i in range(group)])

        return lax.fori_loop(0, nblocks // group, some, total)

    place_rows = lax.broadcasted_iota(jnp.int32, (3, width), 0)

    def walk(step, blocks):
        moves = []
        for j in blocks:
            cells = cell[step : step + 1, pl.ds(pl.multiple_of(j * width, width), width)]
            row_hit = high_bits(cells) == cell_rows
            local = lax.div(tile[step, 0, j], doms)
            both = jnp.concatenate(
                [table[local, slab].reshape(4 * rows, LANES) for slab in (step, step + 1)], axis=0
            )
            found = jnp.dot(both, low_hits(cells), preferred_element_type=F32)
            found = found.reshape(2, 4, rows, width)
            sums = [
                jnp.sum(jnp.where(row_hit, found[0, ch] + found[1, ch], 0.0), axis=0, keepdims=True)
                for ch in range(4)
            ]
            drift = jnp.where(place_rows == 0, sums[0], jnp.where(place_rows == 1, sums[1], sums[2]))
            draw = noise[step, :, pl.ds(pl.multiple_of(j * width, width), width)]
            moves.append(0.5 * time_step * drift + jnp.sqrt(time_step * sums[3]) * draw)
        return moves

    third = (lax.broadcasted_iota(jnp.int32, (3, width), 0) == 2)

    total = jnp.zeros((LANES, 16), F32)

    for copy in staged[7:]:
        copy.wait()
    table_copy.wait_recv()

    def first(k, _):
        blocks = [k * group + i for i in range(group)]
        moves = walk(0, blocks)
        values = []
        for j, move in zip(blocks, moves):
            speed = jnp.concatenate([settle[j, 0:1, :], settle[j, 1:2, :]], axis=1)
            sink = jnp.where(third, steps * time_step * speed, 0.0)
            here = pos[:, pl.ds(pl.multiple_of(j * width, width), width)]
            values.append(here - sink + move)
        for j, value in zip(blocks, values):
            delta[j] = value
        return 0

    lax.fori_loop(0, nblocks // group, first, 0)

    def send_places(step, source):
        def one(p, _):
            pos_send[step][p] = source(inverse[step, lax.rem(me + p, doms)])
            send(step, pos_send, pos_recv, pos_sem, p)
            return 0

        lax.fori_loop(1, doms, one, 0, unroll=5 if doms == 16 else 1)
        pos_recv[step][me] = source(inverse[step, me])

    send_places(0, lambda j: delta[j])

    for step in range(1, steps):
        if step + 1 < steps:
            find_inverse(step)
        def some(k, total, step=step):
            blocks = [k * group + i for i in range(group)]
            moves = walk(step, blocks)
            if step + 1 == steps:
                total = total + sum(deposits(earlier, blocks) for earlier in range(step))
            for j, move in zip(blocks, moves):
                delta[j] = move
            return total

        def forward(step=step):
            whole(step - 1, carried_send, carried_recv, carried_sem).wait_recv()

            def source(j):
                fade = carried_recv[step - 1][j, 2:4, :]
                return carried_recv[step - 1][j, 0:2, :] * fade, fade

            send_carried(step, source)

        if step + 1 < steps:
            forward()
        total = lax.fori_loop(0, nblocks // group, some, total)
        if step + 1 == steps:
            whole(step - 1, carried_send, carried_recv, carried_sem).wait_recv()
        masses = carried_recv[step - 1][:, 0:2, :]
        fade = carried_recv[step - 1][:, 2:4, :]
        left = masses * fade
        dep[step][...] = masses - left
        if step + 1 == steps:
            mass_out[...] = left
            total = all_deposits(step, total)
        if step + 1 == steps:
            total = total.T
            for t in range(archs):
                q = BEDC // LANES
                bed_part[t] = (total[t * q : (t + 1) * q] + total[8 + t * q : 8 + (t + 1) * q]) * scale
            bed_copy = pltpu.make_async_remote_copy(
                src_ref=bed_part.at[twin], dst_ref=bed_recv, send_sem=bed_sem.at[0], recv_sem=bed_sem.at[1],
                device_id={"arch": twin}, device_id_type=MESH,
            )
            bed_copy.start()
        whole(step - 1, pos_send, pos_recv, pos_sem).wait_recv()
        if step + 1 < steps:
            send_places(step, lambda j, step=step: pos_recv[step - 1][j] + delta[j])

    last = steps - 2
    def finish(j, _):
        pos_out[:, pl.ds(pl.multiple_of(j * width, width), width)] = pos_recv[last][j] + delta[j]
        return 0

    lax.fori_loop(0, nblocks, finish, 0, unroll=16)
    bed_copy.wait_recv()
    bed_out[...] = bed_part[arch] + bed_recv[...]

    table_copy.wait_send()
    bed_copy.wait_send()
    for step in range(steps - 1):
        whole(step, carried_send, carried_recv, carried_sem).wait_send()
        whole(step, pos_send, pos_recv, pos_sem).wait_send()


def write_out(*refs):
    count = len(refs) // 2
    sem = refs[-1]
    copies = [pltpu.make_async_copy(refs[i], refs[count + i], sem.at[i]) for i in range(count)]
    for copy in copies:
        copy.start()
    for copy in copies:
        copy.wait()


def body(
    position, particle_mass, settling, walk_noise, velocity, diffusivity, block_tile, cell_index, bed_cell, route_code
):
    doms = lax.axis_size("dom")
    archs = lax.axis_size("arch")
    particles = position.shape[1]
    nblocks = block_tile.shape[2]
    width = particles // nblocks
    steps = cell_index.shape[0]
    slabs, _, _, cells = velocity.shape
    rows = cells // LANES
    half = width // LANES
    moves = steps - 1
    in_hbm = pl.BlockSpec(memory_space=pltpu.HBM)
    in_vmem = pl.BlockSpec(memory_space=pltpu.VMEM)
    vmem = pltpu.VMEM
    args = (
        position,
        particle_mass.reshape(nblocks, half, LANES),
        settling.reshape(nblocks, half, LANES),
        walk_noise,
        velocity.transpose(1, 2, 0, 3).reshape(3, slabs, cells),
        diffusivity.transpose(1, 0, 2).reshape(slabs, cells),
        block_tile,
        cell_index,
        bed_cell,
        route_code,
    )
    results = pl.pallas_call(
        functools.partial(
            kernel, doms, archs, nblocks, width, steps, slabs, rows, BEDC / particles
        ),
        out_shape=(
            pltpu.VMEM((3, particles), F32),
            pltpu.VMEM((nblocks, half, LANES), F32),
            pltpu.VMEM((BEDC // LANES, LANES), F32),
        ),
        in_specs=[in_hbm] * len(args),
        out_specs=(in_vmem, in_vmem, in_vmem),
        scratch_shapes=[
            vmem(args[0].shape, F32),
            vmem(args[1].shape, F32),
            vmem(args[2].shape, F32),
            vmem(args[3].shape, F32),
            vmem(args[4].shape, BF16),
            vmem(args[5].shape, BF16),
            pltpu.SMEM(args[6].shape, jnp.int32),
            vmem(args[7].shape, jnp.int32),
            vmem(args[8].shape, jnp.int32),
            pltpu.SMEM(args[9].shape, jnp.int32),
            vmem((4, slabs * rows, LANES), F32),
            vmem((archs, slabs, 4, rows, LANES), BF16),
            pltpu.SMEM((moves, nblocks), jnp.int32),
            vmem((nblocks, half, LANES), F32),
            [vmem((nblocks, half, LANES), F32)] * steps,
            vmem((nblocks, 3, width), F32),
            [vmem((nblocks, 2 * half, LANES), F32)] * moves,
            [vmem((nblocks, 2 * half, LANES), F32)] * moves,
            [vmem((nblocks, 3, width), F32)] * moves,
            [vmem((nblocks, 3, width), F32)] * moves,
            vmem((archs, BEDC // LANES, LANES), F32),
            vmem((BEDC // LANES, LANES), F32),
            pltpu.SemaphoreType.DMA((len(args),)),
            pltpu.SemaphoreType.DMA((2,)),
            pltpu.SemaphoreType.DMA((moves, 2)),
            pltpu.SemaphoreType.DMA((moves, 2)),
            pltpu.SemaphoreType.DMA((2,)),
        ],
        compiler_params=pltpu.CompilerParams(
            collective_id=0, has_side_effects=True, vmem_limit_bytes=60 * 1024 * 1024
        ),
    )(*args)
    places, masses, beds = pl.pallas_call(
        write_out,
        out_shape=tuple(jax.ShapeDtypeStruct(r.shape, F32) for r in results),
        in_specs=[in_vmem] * 3,
        out_specs=(in_hbm,) * 3,
        scratch_shapes=[pltpu.SemaphoreType.DMA((3,))],
    )(*(pltpu.with_memory_space_constraint(r, pltpu.VMEM) for r in results))
    return places, masses.reshape(particles), beds.reshape(1, BEDC)


def solution(mesh):
    return jax.shard_map(
        body,
        mesh=mesh,
        in_specs=(
            P(None, ("arch", "dom")),
            P(("arch", "dom")),
            P(("arch", "dom")),
            P(None, None, ("arch", "dom")),
            P(None, None, ("arch", "dom"), None),
            P(None, ("arch", "dom"), None),
            P(None, ("arch", "dom"), None),
            P(None, ("arch", "dom")),
            P(None, ("arch", "dom")),
            P(None, ("arch", "dom"), None),
        ),
        out_specs=(P(None, ("arch", "dom")), P(("arch", "dom")), P(("arch", "dom"), None)),
        check_vma=False,
    )
```
